256 devices in a mesh: grp: 16 (over z, core), seq: 16 (over x, y).
Axes of the slice: x: 4, y: 4, z: 8, core: 2. Of those that a mesh axis runs over, the one named last changes fastest.
Arguments:
- signal: bfloat16 [65536, 512], P(('grp', 'seq')), may hold values from -6 to 6
- gating: bfloat16 [65536, 512], P(('grp', 'seq')), may hold values from -6 to 6
- kernel: float32 [65536, 512], P(('grp', 'seq')), may hold values from -0.0234375 to 0.0234375
- bypass: float32 [512], replicated, may hold values from 0.5 to 1.5
Outputs:
- filtered: bfloat16 [65536, 512], P(('grp', 'seq'))
The draws below stay inside these ranges and needn't reach their ends.
All inputs are finite; a program needn't handle non-finite values.
Results may differ from the reference program's by a relative error of at most 0.001.
Values sent between devices are 32-bit elements; how exact they have to be, the bound alone decides.
A program may use at most 64 MiB of HBM per device.

```python
import jax
import jax.numpy as jnp

CHANNELS = 512
TOKENS = 65536


def block_levels(stream_key, extent, cuts, smallest, top_value):
    level, own = 1.0, jax.random.fold_in(stream_key, 6)
    for axis_at, parts in cuts:
        heights = jnp.exp(jax.random.uniform(jax.random.fold_in(own, axis_at), (parts,), jnp.float32, smallest / len(cuts), top_value / len(cuts)))
        level = level * jnp.repeat(heights, extent[axis_at] // parts).reshape([-1 if axis == axis_at else 1 for axis in range(len(extent))])
    return level


def scatter_about(key, dims, deviation, limit, shards=(), dtype=jnp.bfloat16):
    result = jax.random.normal(key, dims, jnp.float32) * deviation
    if len(shards) > 0:
        result = block_levels(key, dims, shards, -0.22, 0.18) * result
    return jnp.clip(result, min=-limit, max=limit).astype(dtype)


def setup_inputs(seed: int = 0) -> dict:
    keys = jax.random.split(jax.random.key(seed), 5)
    return {
        "signal": scatter_about(keys[0], (TOKENS, CHANNELS), 1.0, 6.0, ((0, 256),)),
        "gating": scatter_about(keys[1], (TOKENS, CHANNELS), 1.0, 6.0, ((0, 256),)),
        "kernel": scatter_about(keys[2], (TOKENS, CHANNELS), TOKENS ** -0.5, 0.0234375, ((0, 256),), jnp.float32),
        "bypass": jnp.clip(jax.random.uniform(keys[3], (CHANNELS,), jnp.float32, 0.5, 1.5), 0.5, 1.5),
    }


def reference(signal, gating, kernel, bypass):
    length = signal.shape[0]
    signal_real = signal.astype(jnp.float32)
    spectrum = jnp.fft.rfft(signal_real, n=2 * length, axis=0) * jnp.fft.rfft(kernel, n=2 * length, axis=0)
    conv = jnp.fft.irfft(spectrum, n=2 * length, axis=0)[:length]
    mixed = (conv + bypass[None, :] * signal_real) * gating.astype(jnp.float32)
    return mixed.astype(jnp.bfloat16)
```

```python
import functools

import jax
import jax.numpy as jnp
import ml_dtypes
import numpy as np
from jax import lax
from jax.experimental import pallas as pl
from jax.experimental.pallas import tpu as pltpu
from jax.sharding import PartitionSpec as P

MESH = pl.DeviceIdType.MESH
F32 = jnp.float32
BF16 = jnp.bfloat16
ROWS = 256
CHIPS = 128
TOKENS = 65536


def split_table(table):
    high = table.astype(ml_dtypes.bfloat16)
    low = (table - high.astype(np.float64)).astype(ml_dtypes.bfloat16)
    return high, low


def tables():
    row = np.arange(256)
    core, chip = row // CHIPS, row % CHIPS
    n1 = 32 * (chip // 16) + 16 * core + chip % 16
    index = np.arange(256)
    quarter = 4 * index - 1

    first = 2.0 * np.pi / 1024 * (quarter[:, None] * n1[None, :] % 1024)
    first_high, first_low = split_table(np.concatenate([np.cos(first), -np.sin(first)], axis=0))
    first_all = np.concatenate([first_high, first_low, first_high], axis=1)

    turn = 2.0 * np.pi / (4 * TOKENS) * (quarter[:, None] * index[None, :] % (4 * TOKENS))
    turn_all = np.concatenate([np.cos(turn), -np.sin(turn)], axis=1).astype(np.float32)

    second = 2.0 * np.pi / 256 * (index[:, None] * index[None, :] % 256)
    cos, sin = np.cos(second), np.sin(second)
    forward = np.concatenate(split_table(np.block([[cos, -sin], [sin, cos]])), axis=0)
    backward = np.concatenate(split_table(np.block([[cos, sin], [-sin, cos]])), axis=0)

    last = np.concatenate([np.cos(first.T), -np.sin(first.T)], axis=1) / TOKENS
    last_high, last_low = split_table(last)
    last_all = np.concatenate([last_high, last_low, last_high], axis=1)
    return first_all, turn_all, forward, backward, last_all


def dot(a, b):
    return jnp.dot(a, b, preferred_element_type=F32)


def halves(x):
    high = x.astype(BF16)
    return high, (x - high.astype(F32)).astype(BF16)


def kernel_body(
    sig_hbm, gate_hbm, ker_hbm, byp_ref, first_hbm, turn_hbm, fwd_hbm, bwd_hbm, last_hbm,
    out_ref,
    sig, gate, ker, first, turn, fwd, bwd, last,
    wide, sib_u, sib_k, send, recv, a_buf, b_buf, x_buf, p_buf, c_buf, d_buf, y_buf, y_sib, y_send, y_recv,
    load_sem, sib_send, sib_recv, send_sem, recv_sem, round_sem,
):
    grp, seq = lax.axis_index("grp"), lax.axis_index("seq")
    z, core = grp // 2, grp % 2
    other = 1 - core
    chip = z * 16 + seq
    sibling = (z * 2 + other, seq)

    barrier = pltpu.get_barrier_semaphore()
    pl.semaphore_signal(barrier, inc=1, device_id=sibling, device_id_type=MESH)
    for j in range(1, 8):
        pl.semaphore_signal(barrier, inc=1, device_id=((z + j) % 8 * 2 + core, seq), device_id_type=MESH)
    for j in range(1, 16):
        pl.semaphore_signal(barrier, inc=1, device_id=(grp, (seq + j) % 16), device_id_type=MESH)

    loads = [
        pltpu.make_async_copy(source, target, load_sem.at[i])
        for i, (source, target) in enumerate(
            [
                (ker_hbm, ker), (sig_hbm, sig), (first_hbm, first), (turn_hbm, turn),
                (fwd_hbm, fwd), (bwd_hbm, bwd), (last_hbm, last), (gate_hbm, gate),
            ]
        )
    ]
    for load in loads:
        load.start()
    loads[0].wait()
    loads[1].wait()
    wide[...] = sig[...].astype(F32)

    pl.semaphore_wait(barrier, 23)
    far_lanes = pl.ds(pl.multiple_of(other * 256, 256), 256)
    near_lanes = pl.multiple_of(core * 256, 256)
    swaps = [
        pltpu.make_async_remote_copy(
            src_ref=source.at[:, far_lanes], dst_ref=target, send_sem=sib_send.at[i], recv_sem=sib_recv.at[i],
            device_id=sibling, device_id_type=MESH,
        )
        for i, (source, target) in enumerate([(ker, sib_k), (wide, sib_u)])
    ]
    for swap in swaps:
        swap.start()
    for j in range(1, 8):
        pl.semaphore_signal(round_sem, inc=1, device_id=((z + j) % 8 * 2 + core, seq), device_id_type=MESH)

    def place(block, ab, start):
        send[pl.ds(ab * 1024 + start, CHIPS, stride=8), :] = block.T

    for ab in range(2):
        for half in range(2):
            rows = pl.ds(half * 128, 128)
            lanes = pl.ds(near_lanes + ab * 128, 128)
            place(wide[rows, lanes], ab, 2 * core + half)
            place(ker[rows, lanes], ab, 4 + 2 * core + half)
    swaps[0].wait_recv()
    swaps[1].wait_recv()
    for ab in range(2):
        for half in range(2):
            rows, lanes = pl.ds(half * 128, 128), pl.ds(ab * 128, 128)
            place(sib_u[rows, lanes], ab, 2 * other + half)
            place(sib_k[rows, lanes], ab, 4 + 2 * other + half)
    pl.semaphore_wait(round_sem, 7)

    def spread(source, target, base, sends, receives):
        def step(i, carry):
            to_z, to_x, to_y = (z + i % 8) % 8, (seq // 4 + i // 8 % 4) % 4, (seq % 4 + i // 32) % 4
            to_seq = to_x * 4 + to_y
            to_chip = to_z * 16 + to_seq
            pltpu.make_async_remote_copy(
                src_ref=source.at[pl.ds(pl.multiple_of(base + to_chip * 8, 8), 8)],
                dst_ref=target.at[pl.ds(pl.multiple_of(base + chip * 8, 8), 8)],
                send_sem=sends, recv_sem=receives,
                device_id=(to_z * 2 + core, to_seq), device_id_type=MESH,
            ).start()
            return carry

        lax.fori_loop(1, CHIPS, step, 0)
        own = pl.ds(pl.multiple_of(base + chip * 8, 8), 8)
        target[own, :] = source[own, :]

    def drain(buffer, semaphore):
        slabs = buffer.at[pl.ds(0, (CHIPS - 1) * 8)]
        pltpu.make_async_copy(slabs, slabs, semaphore).wait()

    for ab in range(2):
        spread(send, recv, ab * 1024, send_sem.at[ab], recv_sem.at[ab])

    for load in loads[2:]:
        load.wait()

    y_swaps = []
    for ab in range(2):
        drain(recv, recv_sem.at[ab])

        def rows_of(t):
            top = [recv[pl.ds(ab * 1024 + t + half, CHIPS, stride=8), :] for half in range(2)]
            low = [recv[pl.ds(ab * 1024 + t + 2 + half, CHIPS, stride=8), :] for half in range(2)]
            return jnp.concatenate([jnp.concatenate(top, axis=1), jnp.concatenate(low, axis=1)], axis=0)

        u = rows_of(0).astype(BF16)
        a_buf[:, 0:256] = dot(first[:, 0:512], jnp.concatenate([u, u], axis=0))
        k_high, k_low = halves(rows_of(4))
        a_buf[:, 256:512] = dot(first[...], jnp.concatenate([k_high, k_high, k_low], axis=0))

        @pl.loop(0, 8)
        def _(i):
            rows = pl.ds(pl.multiple_of(i * 32, 32), 32)
            rows_im = pl.ds(pl.multiple_of(256 + i * 32, 32), 32)
            turn_re, turn_im = turn[rows, 0:256], turn[rows, 256:512]
            for which in range(2):
                cols = slice(which * 256, which * 256 + 256)
                re, im = a_buf[rows, cols], a_buf[rows_im, cols]
                to = pl.ds(pl.multiple_of(which * 256 + i * 32, 32), 32)
                high, low = halves(re * turn_re - im * turn_im)
                b_buf[to, 0:256], b_buf[to, 512:768] = high, low
                high, low = halves(re * turn_im + im * turn_re)
                b_buf[to, 256:512], b_buf[to, 768:1024] = high, low

        x_buf[...] = (
            dot(b_buf[:, 0:512], fwd[0:512, :]) + dot(b_buf[:, 512:1024], fwd[0:512, :])
            + dot(b_buf[:, 0:512], fwd[512:1024, :])
        )

        @pl.loop(0, 8)
        def _(i):
            rows = pl.ds(pl.multiple_of(i * 32, 32), 32)
            rows_k = pl.ds(pl.multiple_of(256 + i * 32, 32), 32)
            u_re, u_im = x_buf[rows, 0:256], x_buf[rows, 256:512]
            k_re, k_im = x_buf[rows_k, 0:256], x_buf[rows_k, 256:512]
            high, low = halves(u_re * k_re - u_im * k_im)
            p_buf[rows, 0:256], p_buf[rows, 512:768] = high, low
            high, low = halves(u_re * k_im + u_im * k_re)
            p_buf[rows, 256:512], p_buf[rows, 768:1024] = high, low

        c_buf[...] = (
            dot(p_buf[:, 0:512], bwd[0:512, :]) + dot(p_buf[:, 512:1024], bwd[0:512, :])
            + dot(p_buf[:, 0:512], bwd[512:1024, :])
        )

        @pl.loop(0, 8)
        def _(i):
            rows = pl.ds(pl.multiple_of(i * 32, 32), 32)
            turn_re, turn_im = turn[rows, 0:256], turn[rows, 256:512]
            re, im = c_buf[rows, 0:256], c_buf[rows, 256:512]
            for part, value in enumerate([re * turn_re + im * turn_im, im * turn_re - re * turn_im]):
                high, low = halves(value)
                for at, piece in ((0, high), (512, high), (1024, low)):
                    d_buf[pl.ds(pl.multiple_of(at + part * 256 + i * 32, 32), 32), :] = piece

        y_buf[ab] = dot(last[...], d_buf[...])

        swap = pltpu.make_async_remote_copy(
            src_ref=y_buf.at[ab, pl.ds(pl.multiple_of(other * 128, 128), 128)], dst_ref=y_sib.at[ab],
            send_sem=sib_send.at[2 + ab], recv_sem=sib_recv.at[2 + ab], device_id=sibling, device_id_type=MESH,
        )
        swap.start()
        y_swaps.append(swap)
        for half in range(2):
            y_send[pl.ds(4 * core + 2 * ab + half, CHIPS, stride=8), :] = y_buf[
                ab, pl.ds(pl.multiple_of(core * 128, 128), 128), half * 128 : half * 128 + 128
            ]

    for ab in range(2):
        y_swaps[ab].wait_recv()
        for half in range(2):
            y_send[pl.ds(4 * other + 2 * ab + half, CHIPS, stride=8), :] = y_sib[
                ab, :, half * 128 : half * 128 + 128
            ]
    spread(y_send, y_recv, 0, send_sem.at[2], recv_sem.at[2])
    drain(y_recv, recv_sem.at[2])

    for t in range(8):
        ch, half = t // 2 * 128, t % 2 * 128
        conv = y_recv[pl.ds(t, CHIPS, stride=8), :].T
        at = (slice(half, half + 128), slice(ch, ch + 128))
        mixed = (conv + byp_ref[:, ch : ch + 128] * wide[at]) * gate[at].astype(F32)
        out_ref[at] = mixed.astype(BF16)

    for swap in swaps + y_swaps:
        swap.wait_send()
    for ab in range(2):
        drain(send, send_sem.at[ab])
    drain(y_send, send_sem.at[2])


def on_device(consts, signal, gating, kernel, bypass):
    hbm, vmem = pl.BlockSpec(memory_space=pl.ANY), pl.BlockSpec(memory_space=pltpu.VMEM)
    v = pltpu.VMEM
    scratch = [
        v((256, 512), BF16), v((256, 512), BF16), v((256, 512), F32),
        *[v(c.shape, c.dtype) for c in consts],
        v((256, 512), F32), v((256, 256), F32), v((256, 256), F32),
        v((2048, 128), F32), v((2048, 128), F32),
        v((512, 512), F32), v((512, 1024), BF16), v((512, 512), F32), v((256, 1024), BF16), v((256, 512), F32),
        v((1536, 256), BF16), v((2, 256, 256), F32), v((2, 128, 256), F32), v((1024, 128), F32), v((1024, 128), F32),
        pltpu.SemaphoreType.DMA((8,)), pltpu.SemaphoreType.DMA((4,)), pltpu.SemaphoreType.DMA((4,)),
        pltpu.SemaphoreType.DMA((3,)), pltpu.SemaphoreType.DMA((3,)), pltpu.SemaphoreType.REGULAR,
    ]
    return pl.pallas_call(
        kernel_body,
        out_shape=jax.ShapeDtypeStruct((256, 512), BF16),
        in_specs=[hbm, hbm, hbm, vmem] + [hbm] * 5,
        out_specs=vmem,
        scratch_shapes=scratch,
        compiler_params=pltpu.CompilerParams(
            collective_id=0, has_side_effects=True, vmem_limit_bytes=48 * 1024 * 1024
        ),
        name="hyena",
    )(signal, gating, kernel, bypass.reshape(1, 512), *consts)


def solution(mesh):
    rows = P(("grp", "seq"), None)
    consts = tables()

    def whole(signal, gating, kernel, bypass):
        return jax.shard_map(
            functools.partial(on_device, [jnp.asarray(c) for c in consts]),
            mesh=mesh, in_specs=(rows, rows, rows, P()), out_specs=rows, check_vma=False,
        )(signal, gating, kernel, bypass)

    return whole
```

```python
import functools

import jax
import jax.numpy as jnp
import ml_dtypes
import numpy as np
from jax import lax
from jax.experimental import pallas as pl
from jax.experimental.pallas import tpu as pltpu
from jax.sharding import PartitionSpec as P

MESH = pl.DeviceIdType.MESH
F32 = jnp.float32
BF16 = jnp.bfloat16
ROWS = 256
CHIPS = 128
TOKENS = 65536


def split_table(table):
    high = table.astype(ml_dtypes.bfloat16)
    low = (table - high.astype(np.float64)).astype(ml_dtypes.bfloat16)
    return high, low


def tables():
    row = np.arange(256)
    core, chip = row // CHIPS, row % CHIPS
    n1 = 32 * (chip // 16) + 16 * core + chip % 16
    index = np.arange(256)
    quarter = 4 * index - 1

    first = 2.0 * np.pi / 1024 * (quarter[:, None] * n1[None, :] % 1024)
    first_high, first_low = split_table(np.concatenate([np.cos(first), -np.sin(first)], axis=0))
    first_all = np.concatenate([first_high, first_low, first_high], axis=1)

    turn = 2.0 * np.pi / (4 * TOKENS) * (quarter[:, None] * index[None, :] % (4 * TOKENS))
    turn_all = np.concatenate([np.cos(turn), -np.sin(turn)], axis=1).astype(np.float32)

    second = 2.0 * np.pi / 256 * (index[:, None] * index[None, :] % 256)
    cos, sin = np.cos(second), np.sin(second)
    forward = np.concatenate(split_table(np.block([[cos, -sin], [sin, cos]])), axis=0)
    backward = np.concatenate(split_table(np.block([[cos, sin], [-sin, cos]])), axis=0)

    last = np.concatenate([np.cos(first.T), -np.sin(first.T)], axis=1) / TOKENS
    last_high, last_low = split_table(last)
    last_all = np.concatenate([last_high, last_low, last_high], axis=1)
    return first_all, turn_all, forward, backward, last_all


def dot(a, b):
    return jnp.dot(a, b, preferred_element_type=F32)


def halves(x):
    high = x.astype(BF16)
    return high, (x - high.astype(F32)).astype(BF16)


def kernel_body(
    sig_hbm, gate_hbm, ker_hbm, byp_ref, first_hbm, turn_hbm, fwd_hbm, bwd_hbm, last_hbm,
    out_ref,
    sig, gate, ker, first, turn, fwd, bwd, last,
    wide, sib_u, sib_k, send, recv, a_buf, b_buf, x_buf, p_buf, c_buf, d_buf, y_buf, y_sib, y_send, y_recv,
    load_sem, sib_send, sib_recv, send_sem, recv_sem, round_sem,
):
    grp, seq = lax.axis_index("grp"), lax.axis_index("seq")
    z, core = grp // 2, grp % 2
    other = 1 - core
    chip = z * 16 + seq
    sibling = (z * 2 + other, seq)

    barrier = pltpu.get_barrier_semaphore()
    pl.semaphore_signal(barrier, inc=1, device_id=sibling, device_id_type=MESH)
    for j in range(1, 8):
        pl.semaphore_signal(barrier, inc=1, device_id=((z + j) % 8 * 2 + core, seq), device_id_type=MESH)
    for j in range(1, 16):
        pl.semaphore_signal(barrier, inc=1, device_id=(grp, (seq + j) % 16), device_id_type=MESH)

    loads = [
        pltpu.make_async_copy(source, target, load_sem.at[i])
        for i, (source, target) in enumerate(
            [
                (ker_hbm, ker), (sig_hbm, sig), (first_hbm, first), (turn_hbm, turn),
                (fwd_hbm, fwd), (bwd_hbm, bwd), (last_hbm, last), (gate_hbm, gate),
            ]
        )
    ]
    for load in loads:
        load.start()
    loads[0].wait()
    loads[1].wait()
    wide[...] = sig[...].astype(F32)

    pl.semaphore_wait(barrier, 23)
    far_lanes = pl.ds(pl.multiple_of(other * 256, 256), 256)
    near_lanes = pl.multiple_of(core * 256, 256)
    swaps = [
        pltpu.make_async_remote_copy(
            src_ref=source.at[:, far_lanes], dst_ref=target, send_sem=sib_send.at[i], recv_sem=sib_recv.at[i],
            device_id=sibling, device_id_type=MESH,
        )
        for i, (source, target) in enumerate([(ker, sib_k), (wide, sib_u)])
    ]
    for swap in swaps:
        swap.start()
    for j in range(1, 8):
        pl.semaphore_signal(round_sem, inc=1, device_id=((z + j) % 8 * 2 + core, seq), device_id_type=MESH)

    def place(block, ab, start):
        send[pl.ds(ab * 1024 + start, CHIPS, stride=8), :] = block.T

    for ab in range(2):
        for half in range(2):
            rows = pl.ds(half * 128, 128)
            lanes = pl.ds(near_lanes + ab * 128, 128)
            place(wide[rows, lanes], ab, 2 * core + half)
            place(ker[rows, lanes], ab, 4 + 2 * core + half)
    swaps[0].wait_recv()
    swaps[1].wait_recv()
    for ab in range(2):
        for half in range(2):
            rows, lanes = pl.ds(half * 128, 128), pl.ds(ab * 128, 128)
            place(sib_u[rows, lanes], ab, 2 * other + half)
            place(sib_k[rows, lanes], ab, 4 + 2 * other + half)
    pl.semaphore_wait(round_sem, 7)

    def spread(source, target, base, size, sends, receives):
        def step(i, carry):
            to_z = (z + i) & 7
            to_seq = ((seq + (i >> 3 << 2)) & 12) | ((seq + (i >> 5)) & 3)
            to_chip = to_z * 16 + to_seq
            pltpu.make_async_remote_copy(
                src_ref=source.at[pl.ds(pl.multiple_of(base + to_chip * size, size), size)],
                dst_ref=target.at[pl.ds(pl.multiple_of(base + chip * size, size), size)],
                send_sem=sends, recv_sem=receives,
                device_id=(to_z * 2 + core, to_seq), device_id_type=MESH,
            ).start()
            return carry

        lax.fori_loop(1, CHIPS, step, 0)

    def drain(buffer, size, semaphore):
        slabs = buffer.at[pl.ds(0, (CHIPS - 1) * size)]
        pltpu.make_async_copy(slabs, slabs, semaphore).wait()

    for ab in range(2):
        spread(send, recv, ab * 1024, 8, send_sem.at[ab], recv_sem.at[ab])
        own = pl.ds(pl.multiple_of(ab * 1024 + chip * 8, 8), 8)
        recv[own, :] = send[own, :]

    for load in loads[2:]:
        load.wait()

    def y_swap(ab):
        return pltpu.make_async_remote_copy(
            src_ref=y_buf.at[ab, pl.ds(pl.multiple_of(other * 128, 128), 128)], dst_ref=y_sib.at[ab],
            send_sem=sib_send.at[2 + ab], recv_sem=sib_recv.at[2 + ab], device_id=sibling, device_id_type=MESH,
        )

    @pl.loop(0, 2)
    def _(ab):
        drain(recv, 8, recv_sem.at[ab])
        base = pl.multiple_of(ab * 1024, 1024)

        def rows_of(t):
            top = [recv[pl.ds(base + t + half, CHIPS, stride=8), :] for half in range(2)]
            low = [recv[pl.ds(base + t + 2 + half, CHIPS, stride=8), :] for half in range(2)]
            return jnp.concatenate([jnp.concatenate(top, axis=1), jnp.concatenate(low, axis=1)], axis=0)

        u = rows_of(0).astype(BF16)
        a_buf[:, 0:256] = dot(first[:, 0:512], jnp.concatenate([u, u], axis=0))
        k_high, k_low = halves(rows_of(4))
        a_buf[:, 256:512] = dot(first[...], jnp.concatenate([k_high, k_high, k_low], axis=0))

        for i in range(8):
            rows, rows_im = slice(i * 32, i * 32 + 32), slice(256 + i * 32, 288 + i * 32)
            turn_re, turn_im = turn[rows, 0:256], turn[rows, 256:512]
            for which in range(2):
                cols = slice(which * 256, which * 256 + 256)
                re, im = a_buf[rows, cols], a_buf[rows_im, cols]
                to = slice(which * 256 + i * 32, which * 256 + i * 32 + 32)
                high, low = halves(re * turn_re - im * turn_im)
                b_buf[to, 0:256], b_buf[to, 512:768] = high, low
                high, low = halves(re * turn_im + im * turn_re)
                b_buf[to, 256:512], b_buf[to, 768:1024] = high, low

        x_buf[...] = (
            dot(b_buf[:, 0:512], fwd[0:512, :]) + dot(b_buf[:, 512:1024], fwd[0:512, :])
            + dot(b_buf[:, 0:512], fwd[512:1024, :])
        )

        for i in range(8):
            rows, rows_k = slice(i * 32, i * 32 + 32), slice(256 + i * 32, 288 + i * 32)
            u_re, u_im = x_buf[rows, 0:256], x_buf[rows, 256:512]
            k_re, k_im = x_buf[rows_k, 0:256], x_buf[rows_k, 256:512]
            high, low = halves(u_re * k_re - u_im * k_im)
            p_buf[rows, 0:256], p_buf[rows, 512:768] = high, low
            high, low = halves(u_re * k_im + u_im * k_re)
            p_buf[rows, 256:512], p_buf[rows, 768:1024] = high, low

        c_buf[...] = (
            dot(p_buf[:, 0:512], bwd[0:512, :]) + dot(p_buf[:, 512:1024], bwd[0:512, :])
            + dot(p_buf[:, 0:512], bwd[512:1024, :])
        )

        for i in range(8):
            rows = slice(i * 32, i * 32 + 32)
            turn_re, turn_im = turn[rows, 0:256], turn[rows, 256:512]
            re, im = c_buf[rows, 0:256], c_buf[rows, 256:512]
            for part, value in enumerate([re * turn_re + im * turn_im, im * turn_re - re * turn_im]):
                high, low = halves(value)
                for at, piece in ((0, high), (512, high), (1024, low)):
                    d_buf[at + part * 256 + i * 32 : at + part * 256 + i * 32 + 32, :] = piece

        near = pl.ds(pl.multiple_of(core * 128, 128), 128)
        away = pl.ds(pl.multiple_of(other * 128, 128), 128)
        y_buf[ab, away] = dot(last[away, :], d_buf[...])
        swap = y_swap(ab)
        swap.start()
        y_buf[ab, near] = dot(last[near, :], d_buf[...])
        at = pl.multiple_of(ab * 512, 512)
        for half in range(2):
            y_send[pl.ds(at + 2 * core + half, CHIPS, stride=4), :] = y_buf[ab, near, half * 128 : half * 128 + 128]
        swap.wait_recv()
        for half in range(2):
            y_send[pl.ds(at + 2 * other + half, CHIPS, stride=4), :] = y_sib[ab, :, half * 128 : half * 128 + 128]
        spread(y_send, y_recv, at, 4, send_sem.at[2 + ab], recv_sem.at[2 + ab])
        own = pl.ds(pl.multiple_of(at + chip * 4, 4), 4)
        y_recv[own, :] = y_send[own, :]

    for ab in range(2):
        drain(y_recv, 4, recv_sem.at[2 + ab])
        for t in range(4):
            ch, half = t // 2 * 256 + ab * 128, t % 2 * 128
            conv = y_recv[pl.ds(ab * 512 + t, CHIPS, stride=4), :].T
            at = (slice(half, half + 128), slice(ch, ch + 128))
            mixed = (conv + byp_ref[:, ch : ch + 128] * wide[at]) * gate[at].astype(F32)
            out_ref[at] = mixed.astype(BF16)

    for ab in range(2):
        swaps[ab].wait_send()
        y_swap(ab).wait_send()
        drain(send, 8, send_sem.at[ab])
        drain(y_send, 4, send_sem.at[2 + ab])


def on_device(consts, signal, gating, kernel, bypass):
    hbm, vmem = pl.BlockSpec(memory_space=pltpu.HBM), pl.BlockSpec(memory_space=pltpu.VMEM)
    v = pltpu.VMEM
    scratch = [
        v((256, 512), BF16), v((256, 512), BF16), v((256, 512), F32),
        *[v(c.shape, c.dtype) for c in consts],
        v((256, 512), F32), v((256, 256), F32), v((256, 256), F32),
        v((2048, 128), F32), v((2048, 128), F32),
        v((512, 512), F32), v((512, 1024), BF16), v((512, 512), F32), v((256, 1024), BF16), v((256, 512), F32),
        v((1536, 256), BF16), v((2, 256, 256), F32), v((2, 128, 256), F32), v((1024, 128), F32), v((1024, 128), F32),
        pltpu.SemaphoreType.DMA((8,)), pltpu.SemaphoreType.DMA((4,)), pltpu.SemaphoreType.DMA((4,)),
        pltpu.SemaphoreType.DMA((4,)), pltpu.SemaphoreType.DMA((4,)), pltpu.SemaphoreType.REGULAR,
    ]
    return pl.pallas_call(
        kernel_body,
        out_shape=jax.ShapeDtypeStruct((256, 512), BF16),
        in_specs=[hbm, hbm, hbm, vmem] + [hbm] * 5,
        out_specs=vmem,
        scratch_shapes=scratch,
        compiler_params=pltpu.CompilerParams(
            collective_id=0, has_side_effects=True, vmem_limit_bytes=63 * 1024 * 1024
        ),
        name="hyena",
    )(signal, gating, kernel, bypass.reshape(1, 512), *consts)


def solution(mesh):
    rows = P(("grp", "seq"), None)
    consts = tables()

    def whole(signal, gating, kernel, bypass):
        return jax.shard_map(
            functools.partial(on_device, [jnp.asarray(c) for c in consts]),
            mesh=mesh, in_specs=(rows, rows, rows, P()), out_specs=rows, check_vma=False,
        )(signal, gating, kernel, bypass)

    return whole
```

```python
import functools

import jax
import jax.numpy as jnp
import ml_dtypes
import numpy as np
from jax import lax
from jax.experimental import pallas as pl
from jax.experimental.pallas import tpu as pltpu
from jax.sharding import PartitionSpec as P

MESH = pl.DeviceIdType.MESH
F32 = jnp.float32
BF16 = jnp.bfloat16
ROWS = 256
CHIPS = 128
TOKENS = 65536


def hops(offset):
    dz, dx, dy = offset
    return min(dz, 8 - dz) + min(dx, 4 - dx) + min(dy, 4 - dy)


OFFSETS = [(dz, dx, dy) for dx in range(4) for dy in range(4) for dz in range(8)]
FAR_FIRST = sorted(OFFSETS[1:], key=lambda offset: -hops(offset))


def split_table(table):
    high = table.astype(ml_dtypes.bfloat16)
    low = (table - high.astype(np.float64)).astype(ml_dtypes.bfloat16)
    return high, low


def tables():
    row = np.arange(256)
    core, chip = row // CHIPS, row % CHIPS
    n1 = 32 * (chip // 16) + 16 * core + chip % 16
    index = np.arange(256)
    quarter = 4 * index - 1

    first = 2.0 * np.pi / 1024 * (quarter[:, None] * n1[None, :] % 1024)
    first_high, first_low = split_table(np.concatenate([np.cos(first), -np.sin(first)], axis=0))
    first_all = np.concatenate([first_high, first_low, first_high], axis=1)

    turn = 2.0 * np.pi / (4 * TOKENS) * (quarter[:, None] * index[None, :] % (4 * TOKENS))
    turn_all = np.concatenate([np.cos(turn), -np.sin(turn)], axis=1).astype(np.float32)

    second = 2.0 * np.pi / 256 * (index[:, None] * index[None, :] % 256)
    cos, sin = np.cos(second), np.sin(second)
    forward = np.concatenate(split_table(np.block([[cos, -sin], [sin, cos]])), axis=0)
    backward = np.concatenate(split_table(np.block([[cos, sin], [-sin, cos]])), axis=0)

    last = np.concatenate([np.cos(first.T), -np.sin(first.T)], axis=1) / TOKENS
    last_high, last_low = split_table(last)
    last_all = np.concatenate([last_high, last_low, last_high], axis=1)
    return first_all, turn_all, forward, backward, last_all


def dot(a, b):
    return jnp.dot(a, b, preferred_element_type=F32)


def halves(x):
    high = x.astype(BF16)
    return high, (x - high.astype(F32)).astype(BF16)


def kernel_body(
    sig_hbm, gate_hbm, ker_hbm, byp_hbm, first_hbm, turn_hbm, fwd_hbm, bwd_hbm, last_hbm,
    out_ref,
    sig, gate, ker, byp, first, turn, fwd, bwd, last,
    wide, sib_u, sib_k, send, recv, a_buf, b_buf, x_buf, p_buf, c_buf, d_buf, y_buf, y_sib, y_send, y_recv,
    load_sem, sib_send, sib_recv, send_sem, recv_sem, round_sem,
):
    grp, seq = lax.axis_index("grp"), lax.axis_index("seq")
    z, core = grp // 2, grp % 2
    other = 1 - core
    chip = z * 16 + seq
    sibling = (z * 2 + other, seq)

    barrier = pltpu.get_barrier_semaphore()
    in_line = (4, 3, 5, 2, 6, 1, 7)
    for dz in in_line:
        pl.semaphore_signal(barrier, inc=1, device_id=(((z + dz) & 7) * 2 + core, seq), device_id_type=MESH)
    for dz, dx, dy in FAR_FIRST:
        if dz == 0:
            mate = ((seq + 4 * dx) & 12) | ((seq + dy) & 3)
            pl.semaphore_signal(barrier, inc=1, device_id=(grp, mate), device_id_type=MESH)
    pl.semaphore_signal(barrier, inc=1, device_id=sibling, device_id_type=MESH)

    loads = [
        pltpu.make_async_copy(source, target, load_sem.at[i])
        for i, (source, target) in enumerate(
            [
                (ker_hbm, ker), (sig_hbm, sig), (first_hbm, first), (turn_hbm, turn),
                (fwd_hbm, fwd), (bwd_hbm, bwd), (last_hbm, last), (gate_hbm, gate), (byp_hbm, byp),
            ]
        )
    ]
    for load in loads:
        load.start()
    loads[0].wait()
    loads[1].wait()
    wide[...] = sig[...].astype(F32)

    pl.semaphore_wait(barrier, 23)
    far_lanes = pl.ds(pl.multiple_of(other * 256, 256), 256)
    near_lanes = pl.multiple_of(core * 256, 256)
    swaps = [
        pltpu.make_async_remote_copy(
            src_ref=source.at[:, far_lanes], dst_ref=target, send_sem=sib_send.at[i], recv_sem=sib_recv.at[i],
            device_id=sibling, device_id_type=MESH,
        )
        for i, (source, target) in enumerate([(ker, sib_k), (wide, sib_u)])
    ]
    for swap in swaps:
        swap.start()
    for dz in in_line:
        pl.semaphore_signal(round_sem, inc=1, device_id=(((z + dz) & 7) * 2 + core, seq), device_id_type=MESH)

    def place(block, ab, start):
        send[pl.ds(ab * 1024 + start, CHIPS, stride=8), :] = block.T

    def place_near(ab):
        for half in range(2):
            rows = pl.ds(half * 128, 128)
            lanes = pl.ds(near_lanes + ab * 128, 128)
            place(ker[rows, lanes], ab, 4 + 2 * core + half)
            place(wide[rows, lanes], ab, 2 * core + half)

    def place_sibling(ab, which):
        source, at = ((sib_k, 4), (sib_u, 0))[which]
        for half in range(2):
            rows, lanes = pl.ds(half * 128, 128), pl.ds(ab * 128, 128)
            place(source[rows, lanes], ab, at + 2 * other + half)

    def spread(source, target, base, size, sends, receives):
        for dz, dx, dy in FAR_FIRST:
            to_z = (z + dz) & 7
            to_seq = ((seq + 4 * dx) & 12) | ((seq + dy) & 3)
            to_chip = to_z * 16 + to_seq
            pltpu.make_async_remote_copy(
                src_ref=source.at[pl.ds(pl.multiple_of(base + to_chip * size, size), size)],
                dst_ref=target.at[pl.ds(pl.multiple_of(base + chip * size, size), size)],
                send_sem=sends, recv_sem=receives,
                device_id=(to_z * 2 + core, to_seq), device_id_type=MESH,
            ).start()

    def drain(buffer, size, semaphore):
        slabs = buffer.at[pl.ds(0, (CHIPS - 1) * size)]
        pltpu.make_async_copy(slabs, slabs, semaphore).wait()

    def send_slabs(ab):
        spread(send, recv, ab * 1024, 8, send_sem.at[ab], recv_sem.at[ab])
        own = pl.ds(pl.multiple_of(ab * 1024 + chip * 8, 8), 8)
        recv[own, :] = send[own, :]

    place_near(0)
    place_near(1)
    for which in range(2):
        swaps[which].wait_recv()
        place_sibling(0, which)
    pl.semaphore_wait(round_sem, 7)
    send_slabs(0)
    for which in range(2):
        place_sibling(1, which)
    send_slabs(1)

    for load in loads[2:]:
        load.wait()

    def y_swap(ab):
        return pltpu.make_async_remote_copy(
            src_ref=y_buf.at[ab, pl.ds(pl.multiple_of(other * 128, 128), 128)], dst_ref=y_sib.at[ab],
            send_sem=sib_send.at[2 + ab], recv_sem=sib_recv.at[2 + ab], device_id=sibling, device_id_type=MESH,
        )

    @pl.loop(0, 2)
    def _(ab):
        drain(recv, 8, recv_sem.at[ab])
        base = pl.multiple_of(ab * 1024, 1024)

        def rows_of(t):
            top = [recv[pl.ds(base + t + half, CHIPS, stride=8), :] for half in range(2)]
            low = [recv[pl.ds(base + t + 2 + half, CHIPS, stride=8), :] for half in range(2)]
            return jnp.concatenate([jnp.concatenate(top, axis=1), jnp.concatenate(low, axis=1)], axis=0)

        u = rows_of(0).astype(BF16)
        a_buf[:, 0:256] = dot(first[:, 0:512], jnp.concatenate([u, u], axis=0))
        k_high, k_low = halves(rows_of(4))
        a_buf[:, 256:512] = dot(first[...], jnp.concatenate([k_high, k_high, k_low], axis=0))

        for i in range(8):
            rows, rows_im = slice(i * 32, i * 32 + 32), slice(256 + i * 32, 288 + i * 32)
            turn_re, turn_im = turn[rows, 0:256], turn[rows, 256:512]
            for which in range(2):
                cols = slice(which * 256, which * 256 + 256)
                re, im = a_buf[rows, cols], a_buf[rows_im, cols]
                to = slice(which * 256 + i * 32, which * 256 + i * 32 + 32)
                high, low = halves(re * turn_re - im * turn_im)
                b_buf[to, 0:256], b_buf[to, 512:768] = high, low
                high, low = halves(re * turn_im + im * turn_re)
                b_buf[to, 256:512], b_buf[to, 768:1024] = high, low

        x_buf[...] = (
            dot(b_buf[:, 0:512], fwd[0:512, :]) + dot(b_buf[:, 512:1024], fwd[0:512, :])
            + dot(b_buf[:, 0:512], fwd[512:1024, :])
        )

        for i in range(8):
            rows, rows_k = slice(i * 32, i * 32 + 32), slice(256 + i * 32, 288 + i * 32)
            u_re, u_im = x_buf[rows, 0:256], x_buf[rows, 256:512]
            k_re, k_im = x_buf[rows_k, 0:256], x_buf[rows_k, 256:512]
            high, low = halves(u_re * k_re - u_im * k_im)
            p_buf[rows, 0:256], p_buf[rows, 512:768] = high, low
            high, low = halves(u_re * k_im + u_im * k_re)
            p_buf[rows, 256:512], p_buf[rows, 768:1024] = high, low

        c_buf[...] = (
            dot(p_buf[:, 0:512], bwd[0:512, :]) + dot(p_buf[:, 512:1024], bwd[0:512, :])
            + dot(p_buf[:, 0:512], bwd[512:1024, :])
        )

        for i in range(8):
            rows = slice(i * 32, i * 32 + 32)
            turn_re, turn_im = turn[rows, 0:256], turn[rows, 256:512]
            re, im = c_buf[rows, 0:256], c_buf[rows, 256:512]
            for part, value in enumerate([re * turn_re + im * turn_im, im * turn_re - re * turn_im]):
                high, low = halves(value)
                for at, piece in ((0, high), (512, high), (1024, low)):
                    d_buf[at + part * 256 + i * 32 : at + part * 256 + i * 32 + 32, :] = piece

        factor = byp[core * 256 + ab * CHIPS + chip]

        def u_part(which):
            part = [recv[pl.ds(base + 2 * which + half, CHIPS, stride=8), :] for half in range(2)]
            return jnp.concatenate(part, axis=1)

        near = pl.ds(pl.multiple_of(core * 128, 128), 128)
        away = pl.ds(pl.multiple_of(other * 128, 128), 128)
        y_buf[ab, away] = dot(last[away, :], d_buf[...]) + factor * u_part(other)
        swap = y_swap(ab)
        swap.start()
        y_buf[ab, near] = dot(last[near, :], d_buf[...]) + factor * u_part(core)
        at = pl.multiple_of(ab * 512, 512)
        for half in range(2):
            y_send[pl.ds(at + 2 * core + half, CHIPS, stride=4), :] = y_buf[ab, near, half * 128 : half * 128 + 128]
        swap.wait_recv()
        for half in range(2):
            y_send[pl.ds(at + 2 * other + half, CHIPS, stride=4), :] = y_sib[ab, :, half * 128 : half * 128 + 128]
        spread(y_send, y_recv, at, 4, send_sem.at[2 + ab], recv_sem.at[2 + ab])
        own = pl.ds(pl.multiple_of(at + chip * 4, 4), 4)
        y_recv[own, :] = y_send[own, :]

    for ab in range(2):
        drain(y_recv, 4, recv_sem.at[2 + ab])
        for t in range(4):
            ch, half = t // 2 * 256 + ab * 128, t % 2 * 128
            mixed = y_recv[pl.ds(ab * 512 + t, CHIPS, stride=4), :].T
            at = (slice(half, half + 128), slice(ch, ch + 128))
            out_ref[at] = (mixed * gate[at].astype(F32)).astype(BF16)

    for ab in range(2):
        swaps[ab].wait_send()
        y_swap(ab).wait_send()
        drain(send, 8, send_sem.at[ab])
        drain(y_send, 4, send_sem.at[2 + ab])


def on_device(consts, signal, gating, kernel, bypass):
    hbm, vmem = pl.BlockSpec(memory_space=pltpu.HBM), pl.BlockSpec(memory_space=pltpu.VMEM)
    v = pltpu.VMEM
    scratch = [
        v((256, 512), BF16), v((256, 512), BF16), v((256, 512), F32), pltpu.SMEM((512,), F32),
        *[v(c.shape, c.dtype) for c in consts],
        v((256, 512), F32), v((256, 256), F32), v((256, 256), F32),
        v((2048, 128), F32), v((2048, 128), F32),
        v((512, 512), F32), v((512, 1024), BF16), v((512, 512), F32), v((256, 1024), BF16), v((256, 512), F32),
        v((1536, 256), BF16), v((2, 256, 256), F32), v((2, 128, 256), F32), v((1024, 128), F32), v((1024, 128), F32),
        pltpu.SemaphoreType.DMA((9,)), pltpu.SemaphoreType.DMA((4,)), pltpu.SemaphoreType.DMA((4,)),
        pltpu.SemaphoreType.DMA((4,)), pltpu.SemaphoreType.DMA((4,)), pltpu.SemaphoreType.REGULAR,
    ]
    return pl.pallas_call(
        kernel_body,
        out_shape=jax.ShapeDtypeStruct((256, 512), BF16),
        in_specs=[hbm] * 9,
        out_specs=vmem,
        scratch_shapes=scratch,
        compiler_params=pltpu.CompilerParams(
            collective_id=0, has_side_effects=True, vmem_limit_bytes=63 * 1024 * 1024
        ),
        name="hyena",
    )(signal, gating, kernel, bypass, *consts)


def solution(mesh):
    rows = P(("grp", "seq"), None)
    consts = tables()

    def whole(signal, gating, kernel, bypass):
        return jax.shard_map(
            functools.partial(on_device, [jnp.asarray(c) for c in consts]),
            mesh=mesh, in_specs=(rows, rows, rows, P()), out_specs=rows, check_vma=False,
        )(signal, gating, kernel, bypass)

    return whole
```

```python
import functools

import jax
import jax.numpy as jnp
import ml_dtypes
import numpy as np
from jax import lax
from jax.experimental import pallas as pl
from jax.experimental.pallas import tpu as pltpu
from jax.sharding import PartitionSpec as P

MESH = pl.DeviceIdType.MESH
F32 = jnp.float32
BF16 = jnp.bfloat16
ROWS = 256
CHIPS = 128
TOKENS = 65536


def hops(offset):
    dz, dx, dy = offset
    return min(dz, 8 - dz) + min(dx, 4 - dx) + min(dy, 4 - dy)


OFFSETS = [(dz, dx, dy) for dx in range(4) for dy in range(4) for dz in range(8)]
FAR_FIRST = sorted(OFFSETS[1:], key=lambda offset: -hops(offset))


def split_table(table):
    high = table.astype(ml_dtypes.bfloat16)
    low = (table - high.astype(np.float64)).astype(ml_dtypes.bfloat16)
    return high, low


def tables():
    row = np.arange(256)
    core, chip = row // CHIPS, row % CHIPS
    n1 = 32 * (chip // 16) + 16 * core + chip % 16
    index = np.arange(256)
    quarter = 4 * index - 1

    first = 2.0 * np.pi / 1024 * (quarter[:, None] * n1[None, :] % 1024)
    halved = first.reshape(2, 1, 128, 256)
    first_rows = np.concatenate([np.cos(halved), -np.sin(halved)], axis=1).reshape(512, 256)
    first_high, first_low = split_table(first_rows)
    first_all = np.concatenate([first_high, first_low, first_high], axis=1)

    turn = 2.0 * np.pi / (4 * TOKENS) * (quarter[:, None] * index[None, :] % (4 * TOKENS))
    turn_all = np.concatenate([np.cos(turn), -np.sin(turn)], axis=1).astype(np.float32)

    second = 2.0 * np.pi / 256 * (index[:, None] * index[None, :] % 256)
    cos, sin = np.cos(second), np.sin(second)
    forward = np.concatenate(split_table(np.block([[cos, -sin], [sin, cos]])), axis=0)
    backward = np.concatenate(split_table(np.block([[cos, sin], [-sin, cos]])), axis=0)

    last = np.concatenate([np.cos(first.T), -np.sin(first.T)], axis=1) / TOKENS
    last_high, last_low = split_table(last)
    last_all = np.concatenate([last_high, last_low, last_high], axis=1)
    return first_all, turn_all, forward, backward, last_all


def dot(a, b):
    return jnp.dot(a, b, preferred_element_type=F32)


def halves(x):
    high = x.astype(BF16)
    return high, (x - high.astype(F32)).astype(BF16)


def kernel_body(
    sig_hbm, gate_hbm, ker_hbm, byp_hbm, first_hbm, turn_hbm, fwd_hbm, bwd_hbm, last_hbm,
    out_ref,
    sig, gate, ker, byp, first, turn, fwd, bwd, last,
    wide, sib_u, sib_k, send, recv, a_buf, b_buf, x_buf, p_buf, c_buf, d_buf, y_buf, y_sib, y_send, y_recv,
    load_sem, sib_send, sib_recv, send_sem, recv_sem, round_sem,
):
    grp, seq = lax.axis_index("grp"), lax.axis_index("seq")
    z, core = grp // 2, grp % 2
    other = 1 - core
    chip = z * 16 + seq
    sibling = (z * 2 + other, seq)

    barrier = pltpu.get_barrier_semaphore()
    in_line = (4, 3, 5, 2, 6, 1, 7)
    for dz in in_line:
        pl.semaphore_signal(barrier, inc=1, device_id=(((z + dz) & 7) * 2 + core, seq), device_id_type=MESH)
    for dz, dx, dy in FAR_FIRST:
        if dz == 0:
            mate = ((seq + 4 * dx) & 12) | ((seq + dy) & 3)
            pl.semaphore_signal(barrier, inc=1, device_id=(grp, mate), device_id_type=MESH)
    pl.semaphore_signal(barrier, inc=1, device_id=sibling, device_id_type=MESH)

    loads = [
        pltpu.make_async_copy(source, target, load_sem.at[i])
        for i, (source, target) in enumerate(
            [
                (ker_hbm, ker), (sig_hbm, sig), (first_hbm, first), (turn_hbm, turn),
                (fwd_hbm, fwd), (bwd_hbm, bwd), (last_hbm, last), (gate_hbm, gate), (byp_hbm, byp),
            ]
        )
    ]
    for load in loads:
        load.start()
    loads[0].wait()
    loads[1].wait()
    wide[...] = sig[...].astype(F32)

    pl.semaphore_wait(barrier, 23)
    far_lanes = pl.ds(pl.multiple_of(other * 256, 256), 256)
    near_lanes = pl.multiple_of(core * 256, 256)
    swaps = [
        pltpu.make_async_remote_copy(
            src_ref=source.at[:, far_lanes], dst_ref=target, send_sem=sib_send.at[i], recv_sem=sib_recv.at[i],
            device_id=sibling, device_id_type=MESH,
        )
        for i, (source, target) in enumerate([(ker, sib_k), (wide, sib_u)])
    ]
    for swap in swaps:
        swap.start()
    for dz in in_line:
        pl.semaphore_signal(round_sem, inc=1, device_id=(((z + dz) & 7) * 2 + core, seq), device_id_type=MESH)

    def place(block, ab, start):
        send[pl.ds(ab * 1024 + start, CHIPS, stride=8), :] = block.T

    def place_near(ab):
        for half in range(2):
            rows = pl.ds(half * 128, 128)
            lanes = pl.ds(near_lanes + ab * 128, 128)
            place(ker[rows, lanes], ab, 4 + 2 * core + half)
            place(wide[rows, lanes], ab, 2 * core + half)

    def place_sibling(ab, which):
        source, at = ((sib_k, 4), (sib_u, 0))[which]
        for half in range(2):
            rows, lanes = pl.ds(half * 128, 128), pl.ds(ab * 128, 128)
            place(source[rows, lanes], ab, at + 2 * other + half)

    def spread(source, target, base, size, sends, receives):
        for dz, dx, dy in FAR_FIRST:
            to_z = (z + dz) & 7
            to_seq = ((seq + 4 * dx) & 12) | ((seq + dy) & 3)
            to_chip = to_z * 16 + to_seq
            pltpu.make_async_remote_copy(
                src_ref=source.at[pl.ds(pl.multiple_of(base + to_chip * size, size), size)],
                dst_ref=target.at[pl.ds(pl.multiple_of(base + chip * size, size), size)],
                send_sem=sends, recv_sem=receives,
                device_id=(to_z * 2 + core, to_seq), device_id_type=MESH,
            ).start()

    def drain(buffer, size, semaphore):
        slabs = buffer.at[pl.ds(0, (CHIPS - 1) * size)]
        pltpu.make_async_copy(slabs, slabs, semaphore).wait()

    def send_slabs(ab):
        spread(send, recv, ab * 1024, 8, send_sem.at[ab], recv_sem.at[ab])
        own = pl.ds(pl.multiple_of(ab * 1024 + chip * 8, 8), 8)
        recv[own, :] = send[own, :]

    place_near(0)
    place_near(1)
    for which in range(2):
        swaps[which].wait_recv()
        place_sibling(0, which)
    pl.semaphore_wait(round_sem, 7)
    send_slabs(0)
    for which in range(2):
        place_sibling(1, which)
    send_slabs(1)

    for load in loads[2:]:
        load.wait()

    def y_swap(ab):
        return pltpu.make_async_remote_copy(
            src_ref=y_buf.at[ab, pl.ds(pl.multiple_of(other * 128, 128), 128)], dst_ref=y_sib.at[ab],
            send_sem=sib_send.at[2 + ab], recv_sem=sib_recv.at[2 + ab], device_id=sibling, device_id_type=MESH,
        )

    @pl.loop(0, 2)
    def _(ab):
        drain(recv, 8, recv_sem.at[ab])
        base = pl.multiple_of(ab * 1024, 1024)

        def rows_of(t):
            top = [recv[pl.ds(base + t + half, CHIPS, stride=8), :] for half in range(2)]
            low = [recv[pl.ds(base + t + 2 + half, CHIPS, stride=8), :] for half in range(2)]
            return jnp.concatenate([jnp.concatenate(top, axis=1), jnp.concatenate(low, axis=1)], axis=0)

        u = rows_of(0).astype(BF16)
        u_twice = jnp.concatenate([u, u], axis=0)
        k_high, k_low = halves(rows_of(4))
        k_thrice = jnp.concatenate([k_high, k_high, k_low], axis=0)

        def columns(part):
            at = slice(part * 256, part * 256 + 256)
            a_buf[at, 0:256] = dot(first[at, 0:512], u_twice)
            a_buf[at, 256:512] = dot(first[at, :], k_thrice)

        def twist(part):
            for i in range(0, 128, 32):
                re_rows = slice(part * 256 + i, part * 256 + i + 32)
                im_rows = slice(part * 256 + 128 + i, part * 256 + 160 + i)
                rows = slice(part * 128 + i, part * 128 + i + 32)
                turn_re, turn_im = turn[rows, 0:256], turn[rows, 256:512]
                for which, to in enumerate((re_rows, im_rows)):
                    cols = slice(which * 256, which * 256 + 256)
                    re, im = a_buf[re_rows, cols], a_buf[im_rows, cols]
                    high, low = halves(re * turn_re - im * turn_im)
                    b_buf[to, 0:256], b_buf[to, 512:768] = high, low
                    high, low = halves(re * turn_im + im * turn_re)
                    b_buf[to, 256:512], b_buf[to, 768:1024] = high, low

        def three(data, table, rows):
            high, low = data[rows, 0:512], data[rows, 512:1024]
            return dot(high, table[0:512, :]) + dot(low, table[0:512, :]) + dot(high, table[512:1024, :])

        def product(part):
            for i in range(0, 128, 32):
                u_rows = slice(part * 256 + i, part * 256 + i + 32)
                k_rows = slice(part * 256 + 128 + i, part * 256 + 160 + i)
                to = slice(part * 128 + i, part * 128 + i + 32)
                u_re, u_im = x_buf[u_rows, 0:256], x_buf[u_rows, 256:512]
                k_re, k_im = x_buf[k_rows, 0:256], x_buf[k_rows, 256:512]
                high, low = halves(u_re * k_re - u_im * k_im)
                p_buf[to, 0:256], p_buf[to, 512:768] = high, low
                high, low = halves(u_re * k_im + u_im * k_re)
                p_buf[to, 256:512], p_buf[to, 768:1024] = high, low

        def untwist(part):
            for i in range(part * 128, part * 128 + 128, 32):
                rows = slice(i, i + 32)
                turn_re, turn_im = turn[rows, 0:256], turn[rows, 256:512]
                re, im = c_buf[rows, 0:256], c_buf[rows, 256:512]
                for at, value in ((i, re * turn_re + im * turn_im), (256 + i, im * turn_re - re * turn_im)):
                    high, low = halves(value)
                    d_buf[at : at + 32, :], d_buf[512 + at : 544 + at, :] = high, high
                    d_buf[1024 + at : 1056 + at, :] = low

        columns(0)
        columns(1)
        twist(0)
        x_buf[0:256, :] = three(b_buf, fwd, slice(0, 256))
        twist(1)
        x_buf[256:512, :] = three(b_buf, fwd, slice(256, 512))
        product(0)
        c_buf[0:128, :] = three(p_buf, bwd, slice(0, 128))
        product(1)
        c_buf[128:256, :] = three(p_buf, bwd, slice(128, 256))
        untwist(0)
        untwist(1)

        factor = byp[core * 256 + ab * CHIPS + chip]

        def u_part(which):
            part = [recv[pl.ds(base + 2 * which + half, CHIPS, stride=8), :] for half in range(2)]
            return jnp.concatenate(part, axis=1)

        near = pl.ds(pl.multiple_of(core * 128, 128), 128)
        away = pl.ds(pl.multiple_of(other * 128, 128), 128)
        y_buf[ab, away] = dot(last[away, :], d_buf[...]) + factor * u_part(other)
        swap = y_swap(ab)
        swap.start()
        y_buf[ab, near] = dot(last[near, :], d_buf[...]) + factor * u_part(core)
        at = pl.multiple_of(ab * 512, 512)
        for half in range(2):
            y_send[pl.ds(at + 2 * core + half, CHIPS, stride=4), :] = y_buf[ab, near, half * 128 : half * 128 + 128]
        swap.wait_recv()
        for half in range(2):
            y_send[pl.ds(at + 2 * other + half, CHIPS, stride=4), :] = y_sib[ab, :, half * 128 : half * 128 + 128]
        spread(y_send, y_recv, at, 4, send_sem.at[2 + ab], recv_sem.at[2 + ab])
        own = pl.ds(pl.multiple_of(at + chip * 4, 4), 4)
        y_recv[own, :] = y_send[own, :]

    for ab in range(2):
        drain(y_recv, 4, recv_sem.at[2 + ab])
        for t in range(4):
            ch, half = t // 2 * 256 + ab * 128, t % 2 * 128
            mixed = y_recv[pl.ds(ab * 512 + t, CHIPS, stride=4), :].T
            at = (slice(half, half + 128), slice(ch, ch + 128))
            out_ref[at] = (mixed * gate[at].astype(F32)).astype(BF16)

    for ab in range(2):
        swaps[ab].wait_send()
        y_swap(ab).wait_send()
        drain(send, 8, send_sem.at[ab])
        drain(y_send, 4, send_sem.at[2 + ab])


def on_device(consts, signal, gating, kernel, bypass):
    hbm, vmem = pl.BlockSpec(memory_space=pltpu.HBM), pl.BlockSpec(memory_space=pltpu.VMEM)
    v = pltpu.VMEM
    scratch = [
        v((256, 512), BF16), v((256, 512), BF16), v((256, 512), F32), pltpu.SMEM((512,), F32),
        *[v(c.shape, c.dtype) for c in consts],
        v((256, 512), F32), v((256, 256), F32), v((256, 256), F32),
        v((2048, 128), F32), v((2048, 128), F32),
        v((512, 512), F32), v((512, 1024), BF16), v((512, 512), F32), v((256, 1024), BF16), v((256, 512), F32),
        v((1536, 256), BF16), v((2, 256, 256), F32), v((2, 128, 256), F32), v((1024, 128), F32), v((1024, 128), F32),
        pltpu.SemaphoreType.DMA((9,)), pltpu.SemaphoreType.DMA((4,)), pltpu.SemaphoreType.DMA((4,)),
        pltpu.SemaphoreType.DMA((4,)), pltpu.SemaphoreType.DMA((4,)), pltpu.SemaphoreType.REGULAR,
    ]
    operands = [pltpu.with_memory_space_constraint(x, pltpu.HBM) for x in (signal, gating, kernel, bypass, *consts)]
    return pl.pallas_call(
        kernel_body,
        out_shape=pltpu.VMEM((256, 512), BF16),
        in_specs=[hbm] * 9,
        out_specs=vmem,
        scratch_shapes=scratch,
        compiler_params=pltpu.CompilerParams(
            collective_id=0, has_side_effects=True, vmem_limit_bytes=48 * 1024 * 1024
        ),
        name="hyena",
    )(*operands)


def solution(mesh):
    rows = P(("grp", "seq"), None)
    consts = tables()

    def whole(signal, gating, kernel, bypass):
        return jax.shard_map(
            functools.partial(on_device, [jnp.asarray(c) for c in consts]),
            mesh=mesh, in_specs=(rows, rows, rows, P()), out_specs=rows, check_vma=False,
        )(signal, gating, kernel, bypass)

    return whole
```

```python
import functools

import jax
import jax.numpy as jnp
import ml_dtypes
import numpy as np
from jax import lax
from jax.experimental import pallas as pl
from jax.experimental.pallas import tpu as pltpu
from jax.sharding import PartitionSpec as P

MESH = pl.DeviceIdType.MESH
F32 = jnp.float32
BF16 = jnp.bfloat16
ROWS = 256
CHIPS = 128
TOKENS = 65536


def hops(offset):
    dz, dx, dy = offset
    return min(dz, 8 - dz) + min(dx, 4 - dx) + min(dy, 4 - dy)


OFFSETS = [(dz, dx, dy) for dx in range(4) for dy in range(4) for dz in range(8)]
FAR_FIRST = sorted(OFFSETS[1:], key=lambda offset: -hops(offset))
PLANES = (1, 7, 2, 6, 3, 5, 4)


def split_table(table):
    high = table.astype(ml_dtypes.bfloat16)
    low = (table - high.astype(np.float64)).astype(ml_dtypes.bfloat16)
    return high, low


def tables():
    row = np.arange(256)
    core, chip = row // CHIPS, row % CHIPS
    n1 = 32 * (chip // 16) + 16 * core + chip % 16
    index = np.arange(256)
    quarter = 4 * index - 1

    first = 2.0 * np.pi / 1024 * (quarter[:, None] * n1[None, :] % 1024)
    halved = first.reshape(2, 1, 128, 256)
    first_rows = np.concatenate([np.cos(halved), -np.sin(halved)], axis=1).reshape(512, 256)
    first_high, first_low = split_table(first_rows)
    first_all = np.concatenate([first_high, first_low, first_high], axis=1)

    turn = 2.0 * np.pi / (4 * TOKENS) * (quarter[:, None] * index[None, :] % (4 * TOKENS))
    turn_all = np.concatenate([np.cos(turn), -np.sin(turn)], axis=1).astype(np.float32)

    second = 2.0 * np.pi / 256 * (index[:, None] * index[None, :] % 256)
    cos, sin = np.cos(second), np.sin(second)
    forward = np.concatenate(split_table(np.block([[cos, -sin], [sin, cos]])), axis=0)
    backward = np.concatenate(split_table(np.block([[cos, sin], [-sin, cos]])), axis=0)

    last = np.concatenate([np.cos(first.T), -np.sin(first.T)], axis=1) / TOKENS
    last_high, last_low = split_table(last)
    last_all = np.concatenate([last_high, last_low, last_high], axis=1)
    return first_all, turn_all, forward, backward, last_all


def dot(a, b):
    return jnp.dot(a, b, preferred_element_type=F32)


def halves(x):
    high = x.astype(BF16)
    return high, (x - high.astype(F32)).astype(BF16)


def kernel_body(
    sig_hbm, gate_hbm, ker_hbm, byp_hbm, first_hbm, turn_hbm, fwd_hbm, bwd_hbm, last_hbm,
    out_ref,
    sig, gate, ker, byp, first, turn, fwd, bwd, last,
    wide, sib_u, sib_k, send, recv, a_buf, b_buf, x_buf, p_buf, c_buf, d_buf, y_buf, y_sib, y_send, y_recv,
    load_sem, sib_send, sib_recv, send_sem, recv_sem, plane_sem,
):
    grp, seq = lax.axis_index("grp"), lax.axis_index("seq")
    z, core = grp // 2, grp % 2
    other = 1 - core
    chip = z * 16 + seq
    sibling = (z * 2 + other, seq)

    loads = [
        pltpu.make_async_copy(source, target, load_sem.at[i])
        for i, (source, target) in enumerate(
            [
                (ker_hbm, ker), (sig_hbm, sig), (first_hbm, first), (turn_hbm, turn),
                (fwd_hbm, fwd), (bwd_hbm, bwd), (last_hbm, last), (gate_hbm, gate), (byp_hbm, byp),
            ]
        )
    ]
    for load in loads[:2]:
        load.start()

    barrier = pltpu.get_barrier_semaphore()
    pl.semaphore_signal(barrier, inc=1, device_id=sibling, device_id_type=MESH)
    for dz, dx, dy in FAR_FIRST:
        if dz == 0:
            mate = ((seq + 4 * dx) & 12) | ((seq + dy) & 3)
            pl.semaphore_signal(barrier, inc=1, device_id=(grp, mate), device_id_type=MESH)
    for dz in PLANES:
        pl.semaphore_signal(barrier, inc=1, device_id=(((z + dz) & 7) * 2 + core, seq), device_id_type=MESH)
    for load in loads[2:]:
        load.start()
    loads[0].wait()
    loads[1].wait()
    wide[...] = sig[...].astype(F32)

    pl.semaphore_wait(barrier, 23)
    for dz in PLANES:
        pl.semaphore_signal(
            plane_sem.at[z], inc=1, device_id=(((z + dz) & 7) * 2 + core, seq), device_id_type=MESH
        )
    far_lanes = pl.ds(pl.multiple_of(other * 256, 256), 256)
    near_lanes = pl.multiple_of(core * 256, 256)
    swaps = [
        pltpu.make_async_remote_copy(
            src_ref=source.at[:, far_lanes], dst_ref=target, send_sem=sib_send.at[i], recv_sem=sib_recv.at[i],
            device_id=sibling, device_id_type=MESH,
        )
        for i, (source, target) in enumerate([(ker, sib_k), (wide, sib_u)])
    ]
    for swap in swaps:
        swap.start()

    def place(block, ab, start):
        send[pl.ds(ab * 1024 + start, CHIPS, stride=8), :] = block.T

    def place_near(ab):
        for half in range(2):
            rows = pl.ds(half * 128, 128)
            lanes = pl.ds(near_lanes + ab * 128, 128)
            place(ker[rows, lanes], ab, 4 + 2 * core + half)
            place(wide[rows, lanes], ab, 2 * core + half)

    def place_sibling(ab, which):
        source, at = ((sib_k, 4), (sib_u, 0))[which]
        for half in range(2):
            rows, lanes = pl.ds(half * 128, 128), pl.ds(ab * 128, 128)
            place(source[rows, lanes], ab, at + 2 * other + half)

    def spread(source, target, base, size, sends, receives, offsets=FAR_FIRST):
        for dz, dx, dy in offsets:
            to_z = (z + dz) & 7
            to_seq = ((seq + 4 * dx) & 12) | ((seq + dy) & 3)
            to_chip = to_z * 16 + to_seq
            pltpu.make_async_remote_copy(
                src_ref=source.at[pl.ds(pl.multiple_of(base + to_chip * size, size), size)],
                dst_ref=target.at[pl.ds(pl.multiple_of(base + chip * size, size), size)],
                send_sem=sends, recv_sem=receives,
                device_id=(to_z * 2 + core, to_seq), device_id_type=MESH,
            ).start()

    def drain(buffer, size, semaphore):
        slabs = buffer.at[pl.ds(0, (CHIPS - 1) * size)]
        pltpu.make_async_copy(slabs, slabs, semaphore).wait()

    def send_slabs(ab, offsets):
        spread(send, recv, ab * 1024, 8, send_sem.at[ab], recv_sem.at[ab], offsets)

    def keep_slab(ab):
        own = pl.ds(pl.multiple_of(ab * 1024 + chip * 8, 8), 8)
        recv[own, :] = send[own, :]

    place_near(0)
    place_near(1)
    for which in range(2):
        swaps[which].wait_recv()
        place_sibling(0, which)
    send_slabs(0, [offset for offset in FAR_FIRST if offset[0] == 0])
    for dz in PLANES:
        pl.semaphore_wait(plane_sem.at[(z + dz) & 7], 1)
        send_slabs(0, [offset for offset in FAR_FIRST if offset[0] == dz])
    for which in range(2):
        place_sibling(1, which)
    send_slabs(1, FAR_FIRST)
    keep_slab(0)
    keep_slab(1)

    for load in loads[2:]:
        load.wait()

    def y_swap(ab):
        return pltpu.make_async_remote_copy(
            src_ref=y_buf.at[ab, pl.ds(pl.multiple_of(other * 128, 128), 128)], dst_ref=y_sib.at[ab],
            send_sem=sib_send.at[2 + ab], recv_sem=sib_recv.at[2 + ab], device_id=sibling, device_id_type=MESH,
        )

    @pl.loop(0, 2)
    def _(ab):
        drain(recv, 8, recv_sem.at[ab])
        base = pl.multiple_of(ab * 1024, 1024)

        def rows_of(t):
            top = [recv[pl.ds(base + t + half, CHIPS, stride=8), :] for half in range(2)]
            low = [recv[pl.ds(base + t + 2 + half, CHIPS, stride=8), :] for half in range(2)]
            return jnp.concatenate([jnp.concatenate(top, axis=1), jnp.concatenate(low, axis=1)], axis=0)

        u = rows_of(0).astype(BF16)
        u_twice = jnp.concatenate([u, u], axis=0)
        k_high, k_low = halves(rows_of(4))
        k_thrice = jnp.concatenate([k_high, k_high, k_low], axis=0)

        def columns(part):
            at = slice(part * 256, part * 256 + 256)
            a_buf[at, 0:256] = dot(first[at, 0:512], u_twice)
            a_buf[at, 256:512] = dot(first[at, :], k_thrice)

        def twist(part):
            for i in range(0, 128, 32):
                re_rows = slice(part * 256 + i, part * 256 + i + 32)
                im_rows = slice(part * 256 + 128 + i, part * 256 + 160 + i)
                rows = slice(part * 128 + i, part * 128 + i + 32)
                turn_re, turn_im = turn[rows, 0:256], turn[rows, 256:512]
                for which, to in enumerate((re_rows, im_rows)):
                    cols = slice(which * 256, which * 256 + 256)
                    re, im = a_buf[re_rows, cols], a_buf[im_rows, cols]
                    high, low = halves(re * turn_re - im * turn_im)
                    b_buf[to, 0:256], b_buf[to, 512:768] = high, low
                    high, low = halves(re * turn_im + im * turn_re)
                    b_buf[to, 256:512], b_buf[to, 768:1024] = high, low

        def three(data, table, rows):
            high, low = data[rows, 0:512], data[rows, 512:1024]
            return dot(high, table[0:512, :]) + dot(low, table[0:512, :]) + dot(high, table[512:1024, :])

        def product(part):
            for i in range(0, 128, 32):
                u_rows = slice(part * 256 + i, part * 256 + i + 32)
                k_rows = slice(part * 256 + 128 + i, part * 256 + 160 + i)
                to = slice(part * 128 + i, part * 128 + i + 32)
                u_re, u_im = x_buf[u_rows, 0:256], x_buf[u_rows, 256:512]
                k_re, k_im = x_buf[k_rows, 0:256], x_buf[k_rows, 256:512]
                high, low = halves(u_re * k_re - u_im * k_im)
                p_buf[to, 0:256], p_buf[to, 512:768] = high, low
                high, low = halves(u_re * k_im + u_im * k_re)
                p_buf[to, 256:512], p_buf[to, 768:1024] = high, low

        def untwist(part):
            for i in range(part * 128, part * 128 + 128, 32):
                rows = slice(i, i + 32)
                turn_re, turn_im = turn[rows, 0:256], turn[rows, 256:512]
                re, im = c_buf[rows, 0:256], c_buf[rows, 256:512]
                for at, value in ((i, re * turn_re + im * turn_im), (256 + i, im * turn_re - re * turn_im)):
                    high, low = halves(value)
                    d_buf[at : at + 32, :], d_buf[512 + at : 544 + at, :] = high, high
                    d_buf[1024 + at : 1056 + at, :] = low

        columns(0)
        columns(1)
        twist(0)
        x_buf[0:256, :] = three(b_buf, fwd, slice(0, 256))
        twist(1)
        x_buf[256:512, :] = three(b_buf, fwd, slice(256, 512))
        product(0)
        c_buf[0:128, :] = three(p_buf, bwd, slice(0, 128))
        product(1)
        c_buf[128:256, :] = three(p_buf, bwd, slice(128, 256))
        untwist(0)
        untwist(1)

        factor = byp[core * 256 + ab * CHIPS + chip]

        def u_part(which):
            part = [recv[pl.ds(base + 2 * which + half, CHIPS, stride=8), :] for half in range(2)]
            return jnp.concatenate(part, axis=1)

        near = pl.ds(pl.multiple_of(core * 128, 128), 128)
        away = pl.ds(pl.multiple_of(other * 128, 128), 128)
        y_buf[ab, away] = dot(last[away, :], d_buf[...]) + factor * u_part(other)
        swap = y_swap(ab)
        swap.start()
        y_buf[ab, near] = dot(last[near, :], d_buf[...]) + factor * u_part(core)
        at = pl.multiple_of(ab * 512, 512)
        for half in range(2):
            y_send[pl.ds(at + 2 * core + half, CHIPS, stride=4), :] = y_buf[ab, near, half * 128 : half * 128 + 128]
        swap.wait_recv()
        for half in range(2):
            y_send[pl.ds(at + 2 * other + half, CHIPS, stride=4), :] = y_sib[ab, :, half * 128 : half * 128 + 128]
        spread(y_send, y_recv, at, 4, send_sem.at[2 + ab], recv_sem.at[2 + ab])
        own = pl.ds(pl.multiple_of(at + chip * 4, 4), 4)
        y_recv[own, :] = y_send[own, :]

    for ab in range(2):
        drain(y_recv, 4, recv_sem.at[2 + ab])
        for t in range(4):
            ch, half = t // 2 * 256 + ab * 128, t % 2 * 128
            mixed = y_recv[pl.ds(ab * 512 + t, CHIPS, stride=4), :].T
            at = (slice(half, half + 128), slice(ch, ch + 128))
            out_ref[at] = (mixed * gate[at].astype(F32)).astype(BF16)

    for ab in range(2):
        swaps[ab].wait_send()
        y_swap(ab).wait_send()
        drain(send, 8, send_sem.at[ab])
        drain(y_send, 4, send_sem.at[2 + ab])


def on_device(consts, signal, gating, kernel, bypass):
    hbm, vmem = pl.BlockSpec(memory_space=pltpu.HBM), pl.BlockSpec(memory_space=pltpu.VMEM)
    v = pltpu.VMEM
    scratch = [
        v((256, 512), BF16), v((256, 512), BF16), v((256, 512), F32), pltpu.SMEM((512,), F32),
        *[v(c.shape, c.dtype) for c in consts],
        v((256, 512), F32), v((256, 256), F32), v((256, 256), F32),
        v((2048, 128), F32), v((2048, 128), F32),
        v((512, 512), F32), v((512, 1024), BF16), v((512, 512), F32), v((256, 1024), BF16), v((256, 512), F32),
        v((1536, 256), BF16), v((2, 256, 256), F32), v((2, 128, 256), F32), v((1024, 128), F32), v((1024, 128), F32),
        pltpu.SemaphoreType.DMA((9,)), pltpu.SemaphoreType.DMA((4,)), pltpu.SemaphoreType.DMA((4,)),
        pltpu.SemaphoreType.DMA((4,)), pltpu.SemaphoreType.DMA((4,)), pltpu.SemaphoreType.REGULAR((8,)),
    ]
    operands = [pltpu.with_memory_space_constraint(x, pltpu.HBM) for x in (signal, gating, kernel, bypass, *consts)]
    return pl.pallas_call(
        kernel_body,
        out_shape=pltpu.VMEM((256, 512), BF16),
        in_specs=[hbm] * 9,
        out_specs=vmem,
        scratch_shapes=scratch,
        compiler_params=pltpu.CompilerParams(
            collective_id=0, has_side_effects=True, vmem_limit_bytes=48 * 1024 * 1024
        ),
        name="hyena",
    )(*operands)


def solution(mesh):
    rows = P(("grp", "seq"), None)
    consts = tables()

    def whole(signal, gating, kernel, bypass):
        return jax.shard_map(
            functools.partial(on_device, [jnp.asarray(c) for c in consts]),
            mesh=mesh, in_specs=(rows, rows, rows, P()), out_specs=rows, check_vma=False,
        )(signal, gating, kernel, bypass)

    return whole
```

```python
import functools

import jax
import jax.numpy as jnp
import ml_dtypes
import numpy as np
from jax import lax
from jax.experimental import pallas as pl
from jax.experimental.pallas import tpu as pltpu
from jax.sharding import PartitionSpec as P

MESH = pl.DeviceIdType.MESH
F32 = jnp.float32
BF16 = jnp.bfloat16
ROWS = 256
CHIPS = 128
TOKENS = 65536


def hops(offset):
    dz, dx, dy = offset
    return min(dz, 8 - dz) + min(dx, 4 - dx) + min(dy, 4 - dy)


OFFSETS = [(dz, dx, dy) for dx in range(4) for dy in range(4) for dz in range(8)]
FAR_FIRST = sorted(OFFSETS[1:], key=lambda offset: -hops(offset))


def split_table(table):
    high = table.astype(ml_dtypes.bfloat16)
    low = (table - high.astype(np.float64)).astype(ml_dtypes.bfloat16)
    return high, low


def tables():
    row = np.arange(256)
    core, chip = row // CHIPS, row % CHIPS
    n1 = 32 * (chip // 16) + 16 * core + chip % 16
    index = np.arange(256)
    quarter = 4 * index - 1

    first = 2.0 * np.pi / 1024 * (quarter[:, None] * n1[None, :] % 1024)
    halved = first.reshape(2, 1, 128, 256)
    first_rows = np.concatenate([np.cos(halved), -np.sin(halved)], axis=1).reshape(512, 256)
    first_high, first_low = split_table(first_rows)
    first_all = np.concatenate([first_high, first_low, first_high], axis=1)

    turn = 2.0 * np.pi / (4 * TOKENS) * (quarter[:, None] * index[None, :] % (4 * TOKENS))
    turn_all = np.concatenate([np.cos(turn), -np.sin(turn)], axis=1).astype(np.float32)

    second = 2.0 * np.pi / 256 * (index[:, None] * index[None, :] % 256)
    cos, sin = np.cos(second), np.sin(second)
    forward = np.concatenate(split_table(np.block([[cos, -sin], [sin, cos]])), axis=0)
    backward = np.concatenate(split_table(np.block([[cos, sin], [-sin, cos]])), axis=0)

    last = np.concatenate([np.cos(first.T), -np.sin(first.T)], axis=1) / TOKENS
    last_high, last_low = split_table(last)
    last_all = np.concatenate([last_high, last_low, last_high], axis=1)
    return first_all, turn_all, forward, backward, last_all


def dot(a, b):
    return jnp.dot(a, b, preferred_element_type=F32)


def halves(x):
    high = x.astype(BF16)
    return high, (x - high.astype(F32)).astype(BF16)


def kernel_body(
    sig_hbm, gate_hbm, ker_hbm, byp_hbm, first_hbm, turn_hbm, fwd_hbm, bwd_hbm, last_hbm,
    out_ref,
    sig, gate, ker, byp, first, turn, fwd, bwd, last,
    wide, sib_u, sib_k, post_out, post_in, send, recv, u_mat, k_mat, a_buf, b_buf, x_buf, p_buf, c_buf, d_buf, y_buf, y_sib, y_send, y_recv,
    load_sem, sib_send, sib_recv, send_sem, recv_sem, in_sem,
):
    grp, seq = lax.axis_index("grp"), lax.axis_index("seq")
    z, core = grp // 2, grp % 2
    other = 1 - core
    chip = z * 16 + seq
    sibling = (z * 2 + other, seq)

    barrier = pltpu.get_barrier_semaphore()

    @pl.when(core == 1)
    def _():
        pl.semaphore_signal(barrier, inc=1, device_id=sibling, device_id_type=MESH)

    for dz, dx, dy in FAR_FIRST:
        mate = (((z + dz) & 7) * 2 + core, ((seq + 4 * dx) & 12) | ((seq + dy) & 3))
        pl.semaphore_signal(barrier, inc=1, device_id=mate, device_id_type=MESH)

    loads = [
        pltpu.make_async_copy(source, target, load_sem.at[i])
        for i, (source, target) in enumerate(
            [
                (ker_hbm, ker), (sig_hbm, sig), (first_hbm, first), (turn_hbm, turn),
                (fwd_hbm, fwd), (bwd_hbm, bwd), (last_hbm, last), (gate_hbm, gate), (byp_hbm, byp),
            ]
        )
    ]
    for load in loads:
        load.start()
    loads[0].wait()
    loads[1].wait()
    wide[...] = sig[...].astype(F32)
    near_lanes = pl.multiple_of(core * 256 + 128, 128)
    far_lanes = pl.multiple_of(other * 256 + 128, 128)

    def place(block, ab, start):
        send[pl.ds(ab * 1024 + start, CHIPS, stride=8), :] = block.T

    for half in range(2):
        rows = slice(half * 128, half * 128 + 128)
        for owner in range(2):
            lanes = slice(owner * 256, owner * 256 + 128)
            place(wide[rows, lanes], 0, 2 * owner + half)
            place(ker[rows, lanes], 0, 4 + 2 * owner + half)

    def place_near():
        for half in range(2):
            rows = slice(half * 128, half * 128 + 128)
            place(wide[rows, pl.ds(near_lanes, 128)], 1, 2 * core + half)
            place(ker[rows, pl.ds(near_lanes, 128)], 1, 4 + 2 * core + half)

    def place_sibling():
        for half in range(2):
            rows = slice(half * 128, half * 128 + 128)
            place(sib_u[rows, :], 1, 2 * other + half)
            place(sib_k[rows, :], 1, 4 + 2 * other + half)

    def spread(source, target, base, size, sends, receives, offsets=FAR_FIRST):
        for dz, dx, dy in offsets:
            to_z = (z + dz) & 7
            to_seq = ((seq + 4 * dx) & 12) | ((seq + dy) & 3)
            to_chip = to_z * 16 + to_seq
            pltpu.make_async_remote_copy(
                src_ref=source.at[pl.ds(pl.multiple_of(base + to_chip * size, size), size)],
                dst_ref=target.at[pl.ds(pl.multiple_of(base + chip * size, size), size)],
                send_sem=sends, recv_sem=receives,
                device_id=(to_z * 2 + core, to_seq), device_id_type=MESH,
            ).start()

    def drain(buffer, size, semaphore):
        slabs = buffer.at[pl.ds(0, (CHIPS - 1) * size)]
        pltpu.make_async_copy(slabs, slabs, semaphore).wait()

    def send_slabs(ab, offsets):
        spread(send, recv, ab * 1024, 8, send_sem.at[ab], recv_sem.at[ab], offsets)

    pl.semaphore_wait(barrier, CHIPS - core)

    @pl.when(core == 0)
    def _():
        pl.semaphore_signal(in_sem, inc=1, device_id=sibling, device_id_type=MESH)

    send_slabs(0, FAR_FIRST[:64])

    @pl.when(core == 1)
    def _():
        pl.semaphore_wait(in_sem, 1)

    swaps = [
        pltpu.make_async_remote_copy(
            src_ref=source.at[:, pl.ds(far_lanes, 128)], dst_ref=target, send_sem=sib_send.at[i],
            recv_sem=sib_recv.at[i], device_id=sibling, device_id_type=MESH,
        )
        for i, (source, target) in enumerate([(ker, sib_k), (wide, sib_u)])
    ]
    for swap in swaps:
        swap.start()
    send_slabs(0, FAR_FIRST[64:])
    place_near()
    for swap in swaps:
        swap.wait_recv()
    place_sibling()
    send_slabs(1, FAR_FIRST)
    for ab in range(2):
        own = pl.ds(pl.multiple_of(ab * 1024 + chip * 8, 8), 8)
        recv[own, :] = send[own, :]

    for load in loads[2:]:
        load.wait()

    def y_swap(ab):
        return pltpu.make_async_remote_copy(
            src_ref=y_buf.at[ab, pl.ds(pl.multiple_of(other * 128, 128), 128)], dst_ref=y_sib.at[ab],
            send_sem=sib_send.at[2 + ab], recv_sem=sib_recv.at[2 + ab], device_id=sibling, device_id_type=MESH,
        )

    post_swap = pltpu.make_async_remote_copy(
        src_ref=post_out, dst_ref=post_in, send_sem=sib_send.at[4], recv_sem=sib_recv.at[4],
        device_id=sibling, device_id_type=MESH,
    )

    @pl.loop(0, 2)
    def _(ab):
        drain(recv, 8, recv_sem.at[ab])

        def arrived(t):
            return recv[pl.ds(ab * 1024 + t, CHIPS, stride=8), :]

        def keep(which, half, u, k):
            rows = pl.ds(pl.multiple_of(which * 128, 128), 128)
            low_rows = pl.ds(pl.multiple_of(256 + which * 128, 128), 128)
            lanes = slice(half * 128, half * 128 + 128)
            u_mat[rows, lanes] = u.astype(BF16)
            k_mat[rows, lanes], k_mat[low_rows, lanes] = halves(k)

        @pl.when(ab == 0)
        def _():
            for half in range(2):
                post_out[half * 128 : half * 128 + 128, :] = arrived(2 * other + half)
                post_out[256 + half * 128 : 384 + half * 128, :] = arrived(4 + 2 * other + half)
            post_swap.start()
            for half in range(2):
                keep(core, half, arrived(2 * core + half), arrived(4 + 2 * core + half))
            post_swap.wait_recv()
            for half in range(2):
                from_sibling = slice(half * 128, half * 128 + 128), slice(256 + half * 128, 384 + half * 128)
                keep(other, half, post_in[from_sibling[0], :], post_in[from_sibling[1], :])

        @pl.when(ab == 1)
        def _():
            for which in range(2):
                for half in range(2):
                    keep(which, half, arrived(2 * which + half), arrived(4 + 2 * which + half))

        u = u_mat[...]
        u_twice = jnp.concatenate([u, u], axis=0)
        k_high, k_low = k_mat[0:256, :], k_mat[256:512, :]
        k_thrice = jnp.concatenate([k_high, k_high, k_low], axis=0)

        def columns(part):
            at = slice(part * 256, part * 256 + 256)
            a_buf[at, 0:256] = dot(first[at, 0:512], u_twice)
            a_buf[at, 256:512] = dot(first[at, :], k_thrice)

        def twist(part):
            for i in range(0, 128, 32):
                re_rows = slice(part * 256 + i, part * 256 + i + 32)
                im_rows = slice(part * 256 + 128 + i, part * 256 + 160 + i)
                rows = slice(part * 128 + i, part * 128 + i + 32)
                turn_re, turn_im = turn[rows, 0:256], turn[rows, 256:512]
                for which, to in enumerate((re_rows, im_rows)):
                    cols = slice(which * 256, which * 256 + 256)
                    re, im = a_buf[re_rows, cols], a_buf[im_rows, cols]
                    high, low = halves(re * turn_re - im * turn_im)
                    b_buf[to, 0:256], b_buf[to, 512:768] = high, low
                    high, low = halves(re * turn_im + im * turn_re)
                    b_buf[to, 256:512], b_buf[to, 768:1024] = high, low

        def three(data, table, rows):
            high, low = data[rows, 0:512], data[rows, 512:1024]
            return dot(high, table[0:512, :]) + dot(low, table[0:512, :]) + dot(high, table[512:1024, :])

        def product(part):
            for i in range(0, 128, 32):
                u_rows = slice(part * 256 + i, part * 256 + i + 32)
                k_rows = slice(part * 256 + 128 + i, part * 256 + 160 + i)
                to = slice(part * 128 + i, part * 128 + i + 32)
                u_re, u_im = x_buf[u_rows, 0:256], x_buf[u_rows, 256:512]
                k_re, k_im = x_buf[k_rows, 0:256], x_buf[k_rows, 256:512]
                high, low = halves(u_re * k_re - u_im * k_im)
                p_buf[to, 0:256], p_buf[to, 512:768] = high, low
                high, low = halves(u_re * k_im + u_im * k_re)
                p_buf[to, 256:512], p_buf[to, 768:1024] = high, low

        def untwist(part):
            for i in range(part * 128, part * 128 + 128, 32):
                rows = slice(i, i + 32)
                turn_re, turn_im = turn[rows, 0:256], turn[rows, 256:512]
                re, im = c_buf[rows, 0:256], c_buf[rows, 256:512]
                for at, value in ((i, re * turn_re + im * turn_im), (256 + i, im * turn_re - re * turn_im)):
                    high, low = halves(value)
                    d_buf[at : at + 32, :], d_buf[512 + at : 544 + at, :] = high, high
                    d_buf[1024 + at : 1056 + at, :] = low

        columns(0)
        columns(1)
        twist(0)
        x_buf[0:256, :] = three(b_buf, fwd, slice(0, 256))
        twist(1)
        x_buf[256:512, :] = three(b_buf, fwd, slice(256, 512))
        product(0)
        c_buf[0:128, :] = three(p_buf, bwd, slice(0, 128))
        product(1)
        c_buf[128:256, :] = three(p_buf, bwd, slice(128, 256))
        untwist(0)
        untwist(1)

        factor = byp[core * 256 + ab * CHIPS + chip]

        def u_part(which):
            return u_mat[pl.ds(pl.multiple_of(which * 128, 128), 128), :].astype(F32)

        near = pl.ds(pl.multiple_of(core * 128, 128), 128)
        away = pl.ds(pl.multiple_of(other * 128, 128), 128)
        y_buf[ab, away] = dot(last[away, :], d_buf[...]) + factor * u_part(other)
        swap = y_swap(ab)
        swap.start()
        y_buf[ab, near] = dot(last[near, :], d_buf[...]) + factor * u_part(core)
        at = pl.multiple_of(ab * 512, 512)
        for half in range(2):
            y_send[pl.ds(at + 2 * core + half, CHIPS, stride=4), :] = y_buf[ab, near, half * 128 : half * 128 + 128]
        swap.wait_recv()
        for half in range(2):
            y_send[pl.ds(at + 2 * other + half, CHIPS, stride=4), :] = y_sib[ab, :, half * 128 : half * 128 + 128]
        spread(y_send, y_recv, at, 4, send_sem.at[2 + ab], recv_sem.at[2 + ab])
        own = pl.ds(pl.multiple_of(at + chip * 4, 4), 4)
        y_recv[own, :] = y_send[own, :]

    for ab in range(2):
        drain(y_recv, 4, recv_sem.at[2 + ab])
        for t in range(4):
            ch, half = t // 2 * 256 + ab * 128, t % 2 * 128
            mixed = y_recv[pl.ds(ab * 512 + t, CHIPS, stride=4), :].T
            at = (slice(half, half + 128), slice(ch, ch + 128))
            out_ref[at] = (mixed * gate[at].astype(F32)).astype(BF16)

    post_swap.wait_send()
    for ab in range(2):
        swaps[ab].wait_send()
        y_swap(ab).wait_send()
        drain(send, 8, send_sem.at[ab])
        drain(y_send, 4, send_sem.at[2 + ab])


def on_device(consts, signal, gating, kernel, bypass):
    hbm, vmem = pl.BlockSpec(memory_space=pltpu.HBM), pl.BlockSpec(memory_space=pltpu.VMEM)
    v = pltpu.VMEM
    scratch = [
        v((256, 512), BF16), v((256, 512), BF16), v((256, 512), F32), pltpu.SMEM((512,), F32),
        *[v(c.shape, c.dtype) for c in consts],
        v((256, 512), F32), v((256, 128), F32), v((256, 128), F32), v((512, 128), F32), v((512, 128), F32),
        v((2048, 128), F32), v((2048, 128), F32), v((256, 256), BF16), v((512, 256), BF16),
        v((512, 512), F32), v((512, 1024), BF16), v((512, 512), F32), v((256, 1024), BF16), v((256, 512), F32),
        v((1536, 256), BF16), v((2, 256, 256), F32), v((2, 128, 256), F32), v((1024, 128), F32), v((1024, 128), F32),
        pltpu.SemaphoreType.DMA((9,)), pltpu.SemaphoreType.DMA((5,)), pltpu.SemaphoreType.DMA((5,)),
        pltpu.SemaphoreType.DMA((4,)), pltpu.SemaphoreType.DMA((4,)), pltpu.SemaphoreType.REGULAR,
    ]
    operands = [pltpu.with_memory_space_constraint(x, pltpu.HBM) for x in (signal, gating, kernel, bypass, *consts)]
    return pl.pallas_call(
        kernel_body,
        out_shape=pltpu.VMEM((256, 512), BF16),
        in_specs=[hbm] * 9,
        out_specs=vmem,
        scratch_shapes=scratch,
        compiler_params=pltpu.CompilerParams(
            collective_id=0, has_side_effects=True, vmem_limit_bytes=48 * 1024 * 1024
        ),
        name="hyena",
    )(*operands)


def solution(mesh):
    rows = P(("grp", "seq"), None)
    consts = tables()

    def whole(signal, gating, kernel, bypass):
        return jax.shard_map(
            functools.partial(on_device, [jnp.asarray(c) for c in consts]),
            mesh=mesh, in_specs=(rows, rows, rows, P()), out_specs=rows, check_vma=False,
        )(signal, gating, kernel, bypass)

    return whole
```

```python
import functools

import jax
import jax.numpy as jnp
import ml_dtypes
import numpy as np
from jax import lax
from jax.experimental import pallas as pl
from jax.experimental.pallas import tpu as pltpu
from jax.sharding import PartitionSpec as P

MESH = pl.DeviceIdType.MESH
F32 = jnp.float32
BF16 = jnp.bfloat16
ROWS = 256
CHIPS = 128
TOKENS = 65536


def hops(offset):
    dz, dx, dy = offset
    return min(dz, 8 - dz) + min(dx, 4 - dx) + min(dy, 4 - dy)


OFFSETS = [(dz, dx, dy) for dx in range(4) for dy in range(4) for dz in range(8)]
FAR_FIRST = sorted(OFFSETS[1:], key=lambda offset: -hops(offset))


def split_table(table):
    high = table.astype(ml_dtypes.bfloat16)
    low = (table - high.astype(np.float64)).astype(ml_dtypes.bfloat16)
    return high, low


def tables():
    row = np.arange(256)
    core, chip = row // CHIPS, row % CHIPS
    n1 = 32 * (chip // 16) + 16 * core + chip % 16
    index = np.arange(256)
    quarter = 4 * index - 1

    first = 2.0 * np.pi / 1024 * (quarter[:, None] * n1[None, :] % 1024)
    halved = first.reshape(2, 1, 128, 256)
    first_rows = np.concatenate([np.cos(halved), -np.sin(halved)], axis=1).reshape(512, 256)
    first_high, first_low = split_table(first_rows)
    first_all = np.concatenate([first_high, first_low, first_high], axis=1)

    turn = 2.0 * np.pi / (4 * TOKENS) * (quarter[:, None] * index[None, :] % (4 * TOKENS))
    turn_all = np.concatenate([np.cos(turn), -np.sin(turn)], axis=1).astype(np.float32)

    second = 2.0 * np.pi / 256 * (index[:, None] * index[None, :] % 256)
    cos, sin = np.cos(second), np.sin(second)
    forward = np.concatenate(split_table(np.block([[cos, -sin], [sin, cos]])), axis=0)
    backward = np.concatenate(split_table(np.block([[cos, sin], [-sin, cos]])), axis=0)

    last = np.concatenate([np.cos(first.T), -np.sin(first.T)], axis=1) / TOKENS
    last_high, last_low = split_table(last)
    last_all = np.concatenate([last_high, last_low, last_high], axis=1)
    return first_all, turn_all, forward, backward, last_all


def dot(a, b):
    return jnp.dot(a, b, preferred_element_type=F32)


def halves(x):
    high = x.astype(BF16)
    return high, (x - high.astype(F32)).astype(BF16)


def kernel_body(
    sig_hbm, gate_hbm, ker_hbm, byp_hbm, first_hbm, turn_hbm, fwd_hbm, bwd_hbm, last_hbm,
    out_ref,
    sig, gate, ker, byp, first, turn, fwd, bwd, last,
    wide, sib_u, sib_k, post_out, post_in, send, recv, u_mat, k_mat, a_buf, b_buf, x_buf, p_buf, c_buf, d_buf, y_buf, y_sib, y_send, y_recv,
    load_sem, sib_send, sib_recv, send_sem, recv_sem, in_sem,
):
    grp, seq = lax.axis_index("grp"), lax.axis_index("seq")
    z, core = grp // 2, grp % 2
    other = 1 - core
    chip = z * 16 + seq
    sibling = (z * 2 + other, seq)

    loads = [
        pltpu.make_async_copy(source, target, load_sem.at[i])
        for i, (source, target) in enumerate(
            [
                (ker_hbm, ker), (sig_hbm, sig), (first_hbm, first), (turn_hbm, turn),
                (fwd_hbm, fwd), (bwd_hbm, bwd), (last_hbm, last), (gate_hbm, gate), (byp_hbm, byp),
            ]
        )
    ]
    for load in loads[:2]:
        load.start()
    barrier = pltpu.get_barrier_semaphore()

    @pl.when(core == 1)
    def _():
        pl.semaphore_signal(barrier, inc=1, device_id=sibling, device_id_type=MESH)

    for dz, dx, dy in FAR_FIRST:
        mate = (((z + dz) & 7) * 2 + core, ((seq + 4 * dx) & 12) | ((seq + dy) & 3))
        pl.semaphore_signal(barrier, inc=1, device_id=mate, device_id_type=MESH)

    loads[0].wait()
    loads[1].wait()
    wide[...] = sig[...].astype(F32)
    near_lanes = pl.multiple_of(core * 256 + 128, 128)
    far_lanes = pl.multiple_of(other * 256 + 128, 128)

    def place(block, ab, start):
        send[pl.ds(ab * 1024 + start, CHIPS, stride=8), :] = block.T

    for half in range(2):
        rows = slice(half * 128, half * 128 + 128)
        for owner in range(2):
            lanes = slice(owner * 256, owner * 256 + 128)
            place(wide[rows, lanes], 0, 2 * owner + half)
            place(ker[rows, lanes], 0, 4 + 2 * owner + half)

    def place_near():
        for half in range(2):
            rows = slice(half * 128, half * 128 + 128)
            place(wide[rows, pl.ds(near_lanes, 128)], 1, 2 * core + half)
            place(ker[rows, pl.ds(near_lanes, 128)], 1, 4 + 2 * core + half)

    def place_sibling():
        for half in range(2):
            rows = slice(half * 128, half * 128 + 128)
            place(sib_u[rows, :], 1, 2 * other + half)
            place(sib_k[rows, :], 1, 4 + 2 * other + half)

    def spread(source, target, base, size, sends, receives, offsets=FAR_FIRST):
        for dz, dx, dy in offsets:
            to_z = (z + dz) & 7
            to_seq = ((seq + 4 * dx) & 12) | ((seq + dy) & 3)
            to_chip = to_z * 16 + to_seq
            pltpu.make_async_remote_copy(
                src_ref=source.at[pl.ds(pl.multiple_of(base + to_chip * size, size), size)],
                dst_ref=target.at[pl.ds(pl.multiple_of(base + chip * size, size), size)],
                send_sem=sends, recv_sem=receives,
                device_id=(to_z * 2 + core, to_seq), device_id_type=MESH,
            ).start()

    def drain(buffer, size, semaphore):
        slabs = buffer.at[pl.ds(0, (CHIPS - 1) * size)]
        pltpu.make_async_copy(slabs, slabs, semaphore).wait()

    def send_slabs(ab, offsets):
        spread(send, recv, ab * 1024, 8, send_sem.at[ab], recv_sem.at[ab], offsets)

    pl.semaphore_wait(barrier, CHIPS - core)

    @pl.when(core == 0)
    def _():
        pl.semaphore_signal(in_sem, inc=1, device_id=sibling, device_id_type=MESH)

    send_slabs(0, FAR_FIRST[:64])
    for load in loads[2:]:
        load.start()

    @pl.when(core == 1)
    def _():
        pl.semaphore_wait(in_sem, 1)

    swaps = [
        pltpu.make_async_remote_copy(
            src_ref=source.at[:, pl.ds(far_lanes, 128)], dst_ref=target, send_sem=sib_send.at[i],
            recv_sem=sib_recv.at[i], device_id=sibling, device_id_type=MESH,
        )
        for i, (source, target) in enumerate([(ker, sib_k), (wide, sib_u)])
    ]
    for swap in swaps:
        swap.start()
    send_slabs(0, FAR_FIRST[64:])
    place_near()
    for swap in swaps:
        swap.wait_recv()
    place_sibling()
    send_slabs(1, FAR_FIRST)
    for ab in range(2):
        own = pl.ds(pl.multiple_of(ab * 1024 + chip * 8, 8), 8)
        recv[own, :] = send[own, :]

    for load in loads[2:]:
        load.wait()

    def y_swap(ab):
        return pltpu.make_async_remote_copy(
            src_ref=y_buf.at[ab, pl.ds(pl.multiple_of(other * 128, 128), 128)], dst_ref=y_sib.at[ab],
            send_sem=sib_send.at[2 + ab], recv_sem=sib_recv.at[2 + ab], device_id=sibling, device_id_type=MESH,
        )

    post_swap = pltpu.make_async_remote_copy(
        src_ref=post_out, dst_ref=post_in, send_sem=sib_send.at[4], recv_sem=sib_recv.at[4],
        device_id=sibling, device_id_type=MESH,
    )

    @pl.loop(0, 2)
    def _(ab):
        drain(recv, 8, recv_sem.at[ab])

        def arrived(t):
            return recv[pl.ds(ab * 1024 + t, CHIPS, stride=8), :]

        def keep(which, half, u, k):
            rows = pl.ds(pl.multiple_of(which * 128, 128), 128)
            low_rows = pl.ds(pl.multiple_of(256 + which * 128, 128), 128)
            lanes = slice(half * 128, half * 128 + 128)
            u_mat[rows, lanes] = u.astype(BF16)
            k_mat[rows, lanes], k_mat[low_rows, lanes] = halves(k)

        @pl.when(ab == 0)
        def _():
            for half in range(2):
                post_out[half * 128 : half * 128 + 128, :] = arrived(2 * other + half)
                post_out[256 + half * 128 : 384 + half * 128, :] = arrived(4 + 2 * other + half)
            post_swap.start()
            for half in range(2):
                keep(core, half, arrived(2 * core + half), arrived(4 + 2 * core + half))
            post_swap.wait_recv()
            for half in range(2):
                from_sibling = slice(half * 128, half * 128 + 128), slice(256 + half * 128, 384 + half * 128)
                keep(other, half, post_in[from_sibling[0], :], post_in[from_sibling[1], :])

        @pl.when(ab == 1)
        def _():
            for which in range(2):
                for half in range(2):
                    keep(which, half, arrived(2 * which + half), arrived(4 + 2 * which + half))

        u = u_mat[...]
        u_twice = jnp.concatenate([u, u], axis=0)
        k_high, k_low = k_mat[0:256, :], k_mat[256:512, :]
        k_thrice = jnp.concatenate([k_high, k_high, k_low], axis=0)

        def columns(part):
            at = slice(part * 256, part * 256 + 256)
            a_buf[at, 0:256] = dot(first[at, 0:512], u_twice)
            a_buf[at, 256:512] = dot(first[at, :], k_thrice)

        def twist(part):
            for i in range(0, 128, 32):
                re_rows = slice(part * 256 + i, part * 256 + i + 32)
                im_rows = slice(part * 256 + 128 + i, part * 256 + 160 + i)
                rows = slice(part * 128 + i, part * 128 + i + 32)
                turn_re, turn_im = turn[rows, 0:256], turn[rows, 256:512]
                for which, to in enumerate((re_rows, im_rows)):
                    cols = slice(which * 256, which * 256 + 256)
                    re, im = a_buf[re_rows, cols], a_buf[im_rows, cols]
                    high, low = halves(re * turn_re - im * turn_im)
                    b_buf[to, 0:256], b_buf[to, 512:768] = high, low
                    high, low = halves(re * turn_im + im * turn_re)
                    b_buf[to, 256:512], b_buf[to, 768:1024] = high, low

        def three(data, table, rows):
            high, low = data[rows, 0:512], data[rows, 512:1024]
            return dot(high, table[0:512, :]) + dot(low, table[0:512, :]) + dot(high, table[512:1024, :])

        def product(part):
            for i in range(0, 128, 32):
                u_rows = slice(part * 256 + i, part * 256 + i + 32)
                k_rows = slice(part * 256 + 128 + i, part * 256 + 160 + i)
                to = slice(part * 128 + i, part * 128 + i + 32)
                u_re, u_im = x_buf[u_rows, 0:256], x_buf[u_rows, 256:512]
                k_re, k_im = x_buf[k_rows, 0:256], x_buf[k_rows, 256:512]
                high, low = halves(u_re * k_re - u_im * k_im)
                p_buf[to, 0:256], p_buf[to, 512:768] = high, low
                high, low = halves(u_re * k_im + u_im * k_re)
                p_buf[to, 256:512], p_buf[to, 768:1024] = high, low

        def untwist(part):
            for i in range(part * 128, part * 128 + 128, 32):
                rows = slice(i, i + 32)
                turn_re, turn_im = turn[rows, 0:256], turn[rows, 256:512]
                re, im = c_buf[rows, 0:256], c_buf[rows, 256:512]
                for at, value in ((i, re * turn_re + im * turn_im), (256 + i, im * turn_re - re * turn_im)):
                    high, low = halves(value)
                    d_buf[at : at + 32, :], d_buf[512 + at : 544 + at, :] = high, high
                    d_buf[1024 + at : 1056 + at, :] = low

        columns(0)
        columns(1)
        twist(0)
        x_buf[0:256, :] = three(b_buf, fwd, slice(0, 256))
        twist(1)
        x_buf[256:512, :] = three(b_buf, fwd, slice(256, 512))
        product(0)
        c_buf[0:128, :] = three(p_buf, bwd, slice(0, 128))
        product(1)
        c_buf[128:256, :] = three(p_buf, bwd, slice(128, 256))
        untwist(0)
        untwist(1)

        factor = byp[core * 256 + ab * CHIPS + chip]

        def u_part(which):
            return u_mat[pl.ds(pl.multiple_of(which * 128, 128), 128), :].astype(F32)

        near = pl.ds(pl.multiple_of(core * 128, 128), 128)
        away = pl.ds(pl.multiple_of(other * 128, 128), 128)
        y_buf[ab, away] = dot(last[away, :], d_buf[...]) + factor * u_part(other)
        swap = y_swap(ab)
        swap.start()
        y_buf[ab, near] = dot(last[near, :], d_buf[...]) + factor * u_part(core)
        at = pl.multiple_of(ab * 512, 512)
        for half in range(2):
            y_send[pl.ds(at + 2 * core + half, CHIPS, stride=4), :] = y_buf[ab, near, half * 128 : half * 128 + 128]
        swap.wait_recv()
        for half in range(2):
            y_send[pl.ds(at + 2 * other + half, CHIPS, stride=4), :] = y_sib[ab, :, half * 128 : half * 128 + 128]
        spread(y_send, y_recv, at, 4, send_sem.at[2 + ab], recv_sem.at[2 + ab])
        own = pl.ds(pl.multiple_of(at + chip * 4, 4), 4)
        y_recv[own, :] = y_send[own, :]

    for ab in range(2):
        drain(y_recv, 4, recv_sem.at[2 + ab])
        for t in range(4):
            ch, half = t // 2 * 256 + ab * 128, t % 2 * 128
            mixed = y_recv[pl.ds(ab * 512 + t, CHIPS, stride=4), :].T
            at = (slice(half, half + 128), slice(ch, ch + 128))
            out_ref[at] = (mixed * gate[at].astype(F32)).astype(BF16)

    post_swap.wait_send()
    for ab in range(2):
        swaps[ab].wait_send()
        y_swap(ab).wait_send()
        drain(send, 8, send_sem.at[ab])
        drain(y_send, 4, send_sem.at[2 + ab])


def on_device(consts, signal, gating, kernel, bypass):
    hbm, vmem = pl.BlockSpec(memory_space=pltpu.HBM), pl.BlockSpec(memory_space=pltpu.VMEM)
    v = pltpu.VMEM
    scratch = [
        v((256, 512), BF16), v((256, 512), BF16), v((256, 512), F32), pltpu.SMEM((512,), F32),
        *[v(c.shape, c.dtype) for c in consts],
        v((256, 512), F32), v((256, 128), F32), v((256, 128), F32), v((512, 128), F32), v((512, 128), F32),
        v((2048, 128), F32), v((2048, 128), F32), v((256, 256), BF16), v((512, 256), BF16),
        v((512, 512), F32), v((512, 1024), BF16), v((512, 512), F32), v((256, 1024), BF16), v((256, 512), F32),
        v((1536, 256), BF16), v((2, 256, 256), F32), v((2, 128, 256), F32), v((1024, 128), F32), v((1024, 128), F32),
        pltpu.SemaphoreType.DMA((9,)), pltpu.SemaphoreType.DMA((5,)), pltpu.SemaphoreType.DMA((5,)),
        pltpu.SemaphoreType.DMA((4,)), pltpu.SemaphoreType.DMA((4,)), pltpu.SemaphoreType.REGULAR,
    ]
    operands = [pltpu.with_memory_space_constraint(x, pltpu.HBM) for x in (signal, gating, kernel, bypass, *consts)]
    return pl.pallas_call(
        kernel_body,
        out_shape=pltpu.VMEM((256, 512), BF16),
        in_specs=[hbm] * 9,
        out_specs=vmem,
        scratch_shapes=scratch,
        compiler_params=pltpu.CompilerParams(
            collective_id=0, has_side_effects=True, vmem_limit_bytes=48 * 1024 * 1024
        ),
        name="hyena",
    )(*operands)


def solution(mesh):
    rows = P(("grp", "seq"), None)
    consts = tables()

    def whole(signal, gating, kernel, bypass):
        return jax.shard_map(
            functools.partial(on_device, [jnp.asarray(c) for c in consts]),
            mesh=mesh, in_specs=(rows, rows, rows, P()), out_specs=rows, check_vma=False,
        )(signal, gating, kernel, bypass)

    return whole
```

```python
import functools

import jax
import jax.numpy as jnp
import ml_dtypes
import numpy as np
from jax import lax
from jax.experimental import pallas as pl
from jax.experimental.pallas import tpu as pltpu
from jax.sharding import PartitionSpec as P

MESH = pl.DeviceIdType.MESH
F32 = jnp.float32
BF16 = jnp.bfloat16
ROWS = 256
CHIPS = 128
TOKENS = 65536


def hops(offset):
    dz, dx, dy = offset
    return min(dz, 8 - dz) + min(dx, 4 - dx) + min(dy, 4 - dy)


OFFSETS = [(dz, dx, dy) for dx in range(4) for dy in range(4) for dz in range(8)]
FAR_FIRST = sorted(OFFSETS[1:], key=lambda offset: -hops(offset))


def split_table(table):
    high = table.astype(ml_dtypes.bfloat16)
    low = (table - high.astype(np.float64)).astype(ml_dtypes.bfloat16)
    return high, low


def tables():
    row = np.arange(256)
    core, chip = row // CHIPS, row % CHIPS
    n1 = 32 * (chip // 16) + 16 * core + chip % 16
    index = np.arange(256)
    quarter = 4 * index - 1

    first = 2.0 * np.pi / 1024 * (quarter[:, None] * n1[None, :] % 1024)
    halved = first.reshape(2, 1, 128, 256)
    first_rows = np.concatenate([np.cos(halved), -np.sin(halved)], axis=1).reshape(512, 256)
    first_high, first_low = split_table(first_rows)
    first_all = np.concatenate([first_high, first_low, first_high], axis=1)

    turn = 2.0 * np.pi / (4 * TOKENS) * (quarter[:, None] * index[None, :] % (4 * TOKENS))
    turn_all = np.concatenate([np.cos(turn), -np.sin(turn)], axis=1).astype(np.float32)

    second = 2.0 * np.pi / 256 * (index[:, None] * index[None, :] % 256)
    cos, sin = np.cos(second), np.sin(second)
    forward = np.concatenate(split_table(np.block([[cos, -sin], [sin, cos]])), axis=0)
    backward = np.concatenate(split_table(np.block([[cos, sin], [-sin, cos]])), axis=0)

    last = np.concatenate([np.cos(first.T), -np.sin(first.T)], axis=1) / TOKENS
    last_high, last_low = split_table(last)
    last_all = np.concatenate([last_high, last_low, last_high], axis=1)
    return first_all, turn_all, forward, backward, last_all


def dot(a, b):
    return jnp.dot(a, b, preferred_element_type=F32)


def halves(x):
    high = x.astype(BF16)
    return high, (x - high.astype(F32)).astype(BF16)


def kernel_body(
    sig_hbm, gate_hbm, ker_hbm, byp_hbm, first_hbm, turn_hbm, fwd_hbm, bwd_hbm, last_hbm,
    out_ref,
    sig, gate, ker, byp, first, turn, fwd, bwd, last,
    wide, sib_u, sib_k, post_out, post_in, send, recv, u_mat, k_mat, a_buf, b_buf, x_buf, p_buf, c_buf, d_buf, y_buf, y_out, y_in, y_send, y_recv,
    load_sem, sib_send, sib_recv, send_sem, recv_sem, in_sem,
):
    grp, seq = lax.axis_index("grp"), lax.axis_index("seq")
    z, core = grp // 2, grp % 2
    other = 1 - core
    chip = z * 16 + seq
    sibling = (z * 2 + other, seq)

    loads = [
        pltpu.make_async_copy(source, target, load_sem.at[i])
        for i, (source, target) in enumerate(
            [
                (ker_hbm, ker), (sig_hbm, sig), (first_hbm, first), (turn_hbm, turn),
                (fwd_hbm, fwd), (bwd_hbm, bwd), (last_hbm, last), (gate_hbm, gate), (byp_hbm, byp),
            ]
        )
    ]
    for load in loads[:2]:
        load.start()
    barrier = pltpu.get_barrier_semaphore()

    @pl.when(core == 1)
    def _():
        pl.semaphore_signal(barrier, inc=1, device_id=sibling, device_id_type=MESH)

    for dz, dx, dy in FAR_FIRST:
        mate = (((z + dz) & 7) * 2 + core, ((seq + 4 * dx) & 12) | ((seq + dy) & 3))
        pl.semaphore_signal(barrier, inc=1, device_id=mate, device_id_type=MESH)

    loads[0].wait()
    loads[1].wait()
    wide[...] = sig[...].astype(F32)
    near_lanes = pl.multiple_of(core * 256 + 128, 128)
    far_lanes = pl.multiple_of(other * 256 + 128, 128)

    def place(block, ab, start):
        send[pl.ds(ab * 1024 + start, CHIPS, stride=8), :] = block.T

    for half in range(2):
        rows = slice(half * 128, half * 128 + 128)
        for owner in range(2):
            lanes = slice(owner * 256, owner * 256 + 128)
            place(wide[rows, lanes], 0, 2 * owner + half)
            place(ker[rows, lanes], 0, 4 + 2 * owner + half)

    def place_near():
        for half in range(2):
            rows = slice(half * 128, half * 128 + 128)
            place(wide[rows, pl.ds(near_lanes, 128)], 1, 2 * core + half)
            place(ker[rows, pl.ds(near_lanes, 128)], 1, 4 + 2 * core + half)

    def place_sibling():
        for half in range(2):
            rows = slice(half * 128, half * 128 + 128)
            place(sib_u[rows, :], 1, 2 * other + half)
            place(sib_k[rows, :], 1, 4 + 2 * other + half)

    def spread(source, target, base, size, sends, receives, offsets=FAR_FIRST):
        for dz, dx, dy in offsets:
            to_z = (z + dz) & 7
            to_seq = ((seq + 4 * dx) & 12) | ((seq + dy) & 3)
            to_chip = to_z * 16 + to_seq
            pltpu.make_async_remote_copy(
                src_ref=source.at[pl.ds(pl.multiple_of(base + to_chip * size, size), size)],
                dst_ref=target.at[pl.ds(pl.multiple_of(base + chip * size, size), size)],
                send_sem=sends, recv_sem=receives,
                device_id=(to_z * 2 + core, to_seq), device_id_type=MESH,
            ).start()

    def drain(buffer, size, semaphore):
        slabs = buffer.at[pl.ds(0, (CHIPS - 1) * size)]
        pltpu.make_async_copy(slabs, slabs, semaphore).wait()

    def send_slabs(ab, offsets):
        spread(send, recv, ab * 1024, 8, send_sem.at[ab], recv_sem.at[ab], offsets)

    pl.semaphore_wait(barrier, CHIPS - core)

    @pl.when(core == 0)
    def _():
        pl.semaphore_signal(in_sem, inc=1, device_id=sibling, device_id_type=MESH)

    send_slabs(0, FAR_FIRST[:64])
    for load in loads[2:]:
        load.start()

    @pl.when(core == 1)
    def _():
        pl.semaphore_wait(in_sem, 1)

    swaps = [
        pltpu.make_async_remote_copy(
            src_ref=source.at[:, pl.ds(far_lanes, 128)], dst_ref=target, send_sem=sib_send.at[i],
            recv_sem=sib_recv.at[i], device_id=sibling, device_id_type=MESH,
        )
        for i, (source, target) in enumerate([(ker, sib_k), (wide, sib_u)])
    ]
    for swap in swaps:
        swap.start()
    send_slabs(0, FAR_FIRST[64:])
    place_near()
    for swap in swaps:
        swap.wait_recv()
    place_sibling()
    send_slabs(1, FAR_FIRST)
    for ab in range(2):
        own = pl.ds(pl.multiple_of(ab * 1024 + chip * 8, 8), 8)
        recv[own, :] = send[own, :]

    for load in loads[2:]:
        load.wait()

    def y_swap(ab):
        return pltpu.make_async_remote_copy(
            src_ref=y_out.at[ab], dst_ref=y_in.at[ab],
            send_sem=sib_send.at[2 + ab], recv_sem=sib_recv.at[2 + ab], device_id=sibling, device_id_type=MESH,
        )

    post_swap = pltpu.make_async_remote_copy(
        src_ref=post_out, dst_ref=post_in, send_sem=sib_send.at[4], recv_sem=sib_recv.at[4],
        device_id=sibling, device_id_type=MESH,
    )

    @pl.loop(0, 2)
    def _(ab):
        drain(recv, 8, recv_sem.at[ab])

        def arrived(t):
            return recv[pl.ds(ab * 1024 + t, CHIPS, stride=8), :]

        def keep(which, half, u, k):
            rows = pl.ds(pl.multiple_of(which * 128, 128), 128)
            low_rows = pl.ds(pl.multiple_of(256 + which * 128, 128), 128)
            lanes = slice(half * 128, half * 128 + 128)
            u_mat[rows, lanes] = u.astype(BF16)
            k_mat[rows, lanes], k_mat[low_rows, lanes] = halves(k)

        @pl.when(ab == 0)
        def _():
            for half in range(2):
                post_out[half * 128 : half * 128 + 128, :] = arrived(2 * other + half)
                post_out[256 + half * 128 : 384 + half * 128, :] = arrived(4 + 2 * other + half)
            post_swap.start()
            for half in range(2):
                keep(core, half, arrived(2 * core + half), arrived(4 + 2 * core + half))
            post_swap.wait_recv()
            for half in range(2):
                from_sibling = slice(half * 128, half * 128 + 128), slice(256 + half * 128, 384 + half * 128)
                keep(other, half, post_in[from_sibling[0], :], post_in[from_sibling[1], :])

        @pl.when(ab == 1)
        def _():
            for which in range(2):
                for half in range(2):
                    keep(which, half, arrived(2 * which + half), arrived(4 + 2 * which + half))

        u = u_mat[...]
        u_twice = jnp.concatenate([u, u], axis=0)
        k_high, k_low = k_mat[0:256, :], k_mat[256:512, :]
        k_thrice = jnp.concatenate([k_high, k_high, k_low], axis=0)

        def columns(part):
            at = slice(part * 256, part * 256 + 256)
            a_buf[at, 0:256] = dot(first[at, 0:512], u_twice)
            a_buf[at, 256:512] = dot(first[at, :], k_thrice)

        def twist(part):
            for i in range(0, 128, 32):
                re_rows = slice(part * 256 + i, part * 256 + i + 32)
                im_rows = slice(part * 256 + 128 + i, part * 256 + 160 + i)
                rows = slice(part * 128 + i, part * 128 + i + 32)
                turn_re, turn_im = turn[rows, 0:256], turn[rows, 256:512]
                for which, to in enumerate((re_rows, im_rows)):
                    cols = slice(which * 256, which * 256 + 256)
                    re, im = a_buf[re_rows, cols], a_buf[im_rows, cols]
                    high, low = halves(re * turn_re - im * turn_im)
                    b_buf[to, 0:256], b_buf[to, 512:768] = high, low
                    high, low = halves(re * turn_im + im * turn_re)
                    b_buf[to, 256:512], b_buf[to, 768:1024] = high, low

        def three(data, table, rows):
            high, low = data[rows, 0:512], data[rows, 512:1024]
            return dot(high, table[0:512, :]) + dot(low, table[0:512, :]) + dot(high, table[512:1024, :])

        def product(part):
            for i in range(0, 128, 32):
                u_rows = slice(part * 256 + i, part * 256 + i + 32)
                k_rows = slice(part * 256 + 128 + i, part * 256 + 160 + i)
                to = slice(part * 128 + i, part * 128 + i + 32)
                u_re, u_im = x_buf[u_rows, 0:256], x_buf[u_rows, 256:512]
                k_re, k_im = x_buf[k_rows, 0:256], x_buf[k_rows, 256:512]
                high, low = halves(u_re * k_re - u_im * k_im)
                p_buf[to, 0:256], p_buf[to, 512:768] = high, low
                high, low = halves(u_re * k_im + u_im * k_re)
                p_buf[to, 256:512], p_buf[to, 768:1024] = high, low

        def untwist(part):
            for i in range(part * 128, part * 128 + 128, 32):
                rows = slice(i, i + 32)
                turn_re, turn_im = turn[rows, 0:256], turn[rows, 256:512]
                re, im = c_buf[rows, 0:256], c_buf[rows, 256:512]
                for at, value in ((i, re * turn_re + im * turn_im), (256 + i, im * turn_re - re * turn_im)):
                    high, low = halves(value)
                    d_buf[at : at + 32, :], d_buf[512 + at : 544 + at, :] = high, high
                    d_buf[1024 + at : 1056 + at, :] = low

        columns(0)
        columns(1)
        twist(0)
        x_buf[0:256, :] = three(b_buf, fwd, slice(0, 256))
        twist(1)
        x_buf[256:512, :] = three(b_buf, fwd, slice(256, 512))
        product(0)
        c_buf[0:128, :] = three(p_buf, bwd, slice(0, 128))
        product(1)
        c_buf[128:256, :] = three(p_buf, bwd, slice(128, 256))
        untwist(0)
        untwist(1)

        factor = byp[core * 256 + ab * CHIPS + chip]

        direct = factor * u_mat[...].astype(F32)
        y_buf[...] = dot(last[...], d_buf[...]) + direct
        at = pl.multiple_of(ab * 512, 512)
        for t in range(4):
            which, half = t // 2 * 128, t % 2 * 128
            y_send[pl.ds(at + t, CHIPS, stride=4), :] = y_buf[which : which + 128, half : half + 128]
        spread(y_send, y_recv, at, 4, send_sem.at[2 + ab], recv_sem.at[2 + ab])
        own = pl.ds(pl.multiple_of(at + chip * 4, 4), 4)
        y_recv[own, :] = y_send[own, :]

    def finish(owner, ab, half, values):
        rows, lanes = slice(half * 128, half * 128 + 128), pl.ds(pl.multiple_of(owner * 256 + ab * 128, 128), 128)
        out_ref[rows, lanes] = (values.T * gate[rows, lanes].astype(F32)).astype(BF16)

    for ab in range(2):
        drain(y_recv, 4, recv_sem.at[2 + ab])
        for half in range(2):
            y_out[ab, half * 128 : half * 128 + 128, :] = y_recv[
                pl.ds(ab * 512 + 2 * other + half, CHIPS, stride=4), :
            ]
        y_swap(ab).start()
        for half in range(2):
            finish(core, ab, half, y_recv[pl.ds(ab * 512 + 2 * core + half, CHIPS, stride=4), :])
        y_swap(ab).wait_recv()
        for half in range(2):
            finish(other, ab, half, y_in[ab, half * 128 : half * 128 + 128, :])

    post_swap.wait_send()
    for ab in range(2):
        swaps[ab].wait_send()
        y_swap(ab).wait_send()
        drain(send, 8, send_sem.at[ab])
        drain(y_send, 4, send_sem.at[2 + ab])


def on_device(consts, signal, gating, kernel, bypass):
    hbm, vmem = pl.BlockSpec(memory_space=pltpu.HBM), pl.BlockSpec(memory_space=pltpu.VMEM)
    v = pltpu.VMEM
    scratch = [
        v((256, 512), BF16), v((256, 512), BF16), v((256, 512), F32), pltpu.SMEM((512,), F32),
        *[v(c.shape, c.dtype) for c in consts],
        v((256, 512), F32), v((256, 128), F32), v((256, 128), F32), v((512, 128), F32), v((512, 128), F32),
        v((2048, 128), F32), v((2048, 128), F32), v((256, 256), BF16), v((512, 256), BF16),
        v((512, 512), F32), v((512, 1024), BF16), v((512, 512), F32), v((256, 1024), BF16), v((256, 512), F32),
        v((1536, 256), BF16), v((256, 256), F32), v((2, 256, 128), F32), v((2, 256, 128), F32), v((1024, 128), F32), v((1024, 128), F32),
        pltpu.SemaphoreType.DMA((9,)), pltpu.SemaphoreType.DMA((5,)), pltpu.SemaphoreType.DMA((5,)),
        pltpu.SemaphoreType.DMA((4,)), pltpu.SemaphoreType.DMA((4,)), pltpu.SemaphoreType.REGULAR,
    ]
    operands = [pltpu.with_memory_space_constraint(x, pltpu.HBM) for x in (signal, gating, kernel, bypass, *consts)]
    return pl.pallas_call(
        kernel_body,
        out_shape=pltpu.VMEM((256, 512), BF16),
        in_specs=[hbm] * 9,
        out_specs=vmem,
        scratch_shapes=scratch,
        compiler_params=pltpu.CompilerParams(
            collective_id=0, has_side_effects=True, vmem_limit_bytes=48 * 1024 * 1024
        ),
        name="hyena",
    )(*operands)


def solution(mesh):
    rows = P(("grp", "seq"), None)
    consts = tables()

    def whole(signal, gating, kernel, bypass):
        return jax.shard_map(
            functools.partial(on_device, [jnp.asarray(c) for c in consts]),
            mesh=mesh, in_specs=(rows, rows, rows, P()), out_specs=rows, check_vma=False,
        )(signal, gating, kernel, bypass)

    return whole
```

```python
import functools

import jax
import jax.numpy as jnp
import ml_dtypes
import numpy as np
from jax import lax
from jax.experimental import pallas as pl
from jax.experimental.pallas import tpu as pltpu
from jax.sharding import PartitionSpec as P

MESH = pl.DeviceIdType.MESH
F32 = jnp.float32
BF16 = jnp.bfloat16
ROWS = 256
CHIPS = 128
TOKENS = 65536


def hops(offset):
    dz, dx, dy = offset
    return min(dz, 8 - dz) + min(dx, 4 - dx) + min(dy, 4 - dy)


OFFSETS = [(dz, dx, dy) for dx in range(4) for dy in range(4) for dz in range(8)]
FAR_FIRST = sorted(OFFSETS[1:], key=lambda offset: -hops(offset))


def split_table(table):
    high = table.astype(ml_dtypes.bfloat16)
    low = (table - high.astype(np.float64)).astype(ml_dtypes.bfloat16)
    return high, low


def tables():
    row = np.arange(256)
    core, chip = row // CHIPS, row % CHIPS
    n1 = 32 * (chip // 16) + 16 * core + chip % 16
    index = np.arange(256)
    quarter = 4 * index - 1

    first = 2.0 * np.pi / 1024 * (quarter[:, None] * n1[None, :] % 1024)
    halved = first.reshape(2, 1, 128, 256)
    first_rows = np.concatenate([np.cos(halved), -np.sin(halved)], axis=1).reshape(512, 256)
    first_high, first_low = split_table(first_rows)
    first_all = np.concatenate([first_high, first_low, first_high], axis=1)

    turn = 2.0 * np.pi / (4 * TOKENS) * (quarter[:, None] * index[None, :] % (4 * TOKENS))
    turn_all = np.concatenate([np.cos(turn), -np.sin(turn)], axis=1).astype(np.float32)

    second = 2.0 * np.pi / 256 * (index[:, None] * index[None, :] % 256)
    cos, sin = np.cos(second), np.sin(second)
    forward = np.concatenate(split_table(np.block([[cos, -sin], [sin, cos]])), axis=0)
    backward = np.concatenate(split_table(np.block([[cos, sin], [-sin, cos]])), axis=0)

    last = np.concatenate([np.cos(first.T), -np.sin(first.T)], axis=1) / TOKENS
    last_high, last_low = split_table(last)
    last_all = np.concatenate([last_high, last_low, last_high], axis=1)
    return first_all, turn_all, forward, backward, last_all


def dot(a, b):
    return jnp.dot(a, b, preferred_element_type=F32)


def halves(x):
    high = x.astype(BF16)
    return high, (x - high.astype(F32)).astype(BF16)


def kernel_body(
    sig_hbm, gate_hbm, ker_hbm, byp_hbm, first_hbm, turn_hbm, fwd_hbm, bwd_hbm, last_hbm,
    out_ref,
    sig, gate, ker, byp, first, turn, fwd, bwd, last,
    wide, sib_u, sib_k, post_out, post_in, send, recv, u_mat, k_mat, a_buf, b_buf, x_buf, p_buf, c_buf, d_buf, y_buf, y_out, y_in, y_send, y_recv,
    load_sem, sib_send, sib_recv, send_sem, recv_sem, in_sem,
):
    grp, seq = lax.axis_index("grp"), lax.axis_index("seq")
    z, core = grp // 2, grp % 2
    other = 1 - core
    way = 1 - 2 * core
    chip = z * 16 + seq
    sibling = (z * 2 + other, seq)

    loads = [
        pltpu.make_async_copy(source, target, load_sem.at[i])
        for i, (source, target) in enumerate(
            [
                (ker_hbm, ker), (sig_hbm, sig), (first_hbm, first), (turn_hbm, turn),
                (fwd_hbm, fwd), (bwd_hbm, bwd), (last_hbm, last), (gate_hbm, gate), (byp_hbm, byp),
            ]
        )
    ]
    for load in loads[:2]:
        load.start()
    barrier = pltpu.get_barrier_semaphore()

    @pl.when(core == 1)
    def _():
        pl.semaphore_signal(barrier, inc=1, device_id=sibling, device_id_type=MESH)

    for dz, dx, dy in FAR_FIRST:
        mate = (((z + dz) & 7) * 2 + core, ((seq + 4 * dx) & 12) | ((seq + dy) & 3))
        pl.semaphore_signal(barrier, inc=1, device_id=mate, device_id_type=MESH)

    loads[0].wait()
    loads[1].wait()
    wide[...] = sig[...].astype(F32)
    near_lanes = pl.multiple_of(core * 256 + 128, 128)
    far_lanes = pl.multiple_of(other * 256 + 128, 128)

    def place(block, ab, start):
        send[pl.ds(ab * 1024 + start, CHIPS, stride=8), :] = block.T

    for half in range(2):
        rows = slice(half * 128, half * 128 + 128)
        for owner in range(2):
            lanes = slice(owner * 256, owner * 256 + 128)
            place(wide[rows, lanes], 0, 2 * owner + half)
            place(ker[rows, lanes], 0, 4 + 2 * owner + half)

    def place_near():
        for half in range(2):
            rows = slice(half * 128, half * 128 + 128)
            place(wide[rows, pl.ds(near_lanes, 128)], 1, 2 * core + half)
            place(ker[rows, pl.ds(near_lanes, 128)], 1, 4 + 2 * core + half)

    def place_sibling():
        for half in range(2):
            rows = slice(half * 128, half * 128 + 128)
            place(sib_u[rows, :], 1, 2 * other + half)
            place(sib_k[rows, :], 1, 4 + 2 * other + half)

    def spread(source, target, base, size, sends, receives, offsets=FAR_FIRST):
        for dz, dx, dy in offsets:
            to_z = (z + way * dz) & 7
            to_seq = ((seq + 4 * way * dx) & 12) | ((seq + way * dy) & 3)
            to_chip = to_z * 16 + to_seq
            pltpu.make_async_remote_copy(
                src_ref=source.at[pl.ds(pl.multiple_of(base + to_chip * size, size), size)],
                dst_ref=target.at[pl.ds(pl.multiple_of(base + chip * size, size), size)],
                send_sem=sends, recv_sem=receives,
                device_id=(to_z * 2 + core, to_seq), device_id_type=MESH,
            ).start()

    def drain(buffer, size, semaphore):
        slabs = buffer.at[pl.ds(0, (CHIPS - 1) * size)]
        pltpu.make_async_copy(slabs, slabs, semaphore).wait()

    def send_slabs(ab, offsets):
        spread(send, recv, ab * 1024, 8, send_sem.at[ab], recv_sem.at[ab], offsets)

    pl.semaphore_wait(barrier, CHIPS - core)

    @pl.when(core == 0)
    def _():
        pl.semaphore_signal(in_sem, inc=1, device_id=sibling, device_id_type=MESH)

    send_slabs(0, FAR_FIRST[:64])
    for load in loads[2:]:
        load.start()

    @pl.when(core == 1)
    def _():
        pl.semaphore_wait(in_sem, 1)

    swaps = [
        pltpu.make_async_remote_copy(
            src_ref=source.at[:, pl.ds(far_lanes, 128)], dst_ref=target, send_sem=sib_send.at[i],
            recv_sem=sib_recv.at[i], device_id=sibling, device_id_type=MESH,
        )
        for i, (source, target) in enumerate([(ker, sib_k), (wide, sib_u)])
    ]
    for swap in swaps:
        swap.start()
    send_slabs(0, FAR_FIRST[64:])
    place_near()
    for swap in swaps:
        swap.wait_recv()
    place_sibling()
    send_slabs(1, FAR_FIRST)
    for ab in range(2):
        own = pl.ds(pl.multiple_of(ab * 1024 + chip * 8, 8), 8)
        recv[own, :] = send[own, :]

    for load in loads[2:]:
        load.wait()

    def y_swap(ab):
        return pltpu.make_async_remote_copy(
            src_ref=y_out.at[ab], dst_ref=y_in.at[ab],
            send_sem=sib_send.at[2 + ab], recv_sem=sib_recv.at[2 + ab], device_id=sibling, device_id_type=MESH,
        )

    post_swap = pltpu.make_async_remote_copy(
        src_ref=post_out, dst_ref=post_in, send_sem=sib_send.at[4], recv_sem=sib_recv.at[4],
        device_id=sibling, device_id_type=MESH,
    )

    @pl.loop(0, 2)
    def _(ab):
        drain(recv, 8, recv_sem.at[ab])

        def arrived(t):
            return recv[pl.ds(ab * 1024 + t, CHIPS, stride=8), :]

        def keep(which, half, u, k):
            rows = pl.ds(pl.multiple_of(which * 128, 128), 128)
            low_rows = pl.ds(pl.multiple_of(256 + which * 128, 128), 128)
            lanes = slice(half * 128, half * 128 + 128)
            u_mat[rows, lanes] = u.astype(BF16)
            k_mat[rows, lanes], k_mat[low_rows, lanes] = halves(k)

        @pl.when(ab == 0)
        def _():
            for half in range(2):
                post_out[half * 128 : half * 128 + 128, :] = arrived(2 * other + half)
                post_out[256 + half * 128 : 384 + half * 128, :] = arrived(4 + 2 * other + half)
            post_swap.start()
            for half in range(2):
                keep(core, half, arrived(2 * core + half), arrived(4 + 2 * core + half))
            post_swap.wait_recv()
            for half in range(2):
                from_sibling = slice(half * 128, half * 128 + 128), slice(256 + half * 128, 384 + half * 128)
                keep(other, half, post_in[from_sibling[0], :], post_in[from_sibling[1], :])

        @pl.when(ab == 1)
        def _():
            for which in range(2):
                for half in range(2):
                    keep(which, half, arrived(2 * which + half), arrived(4 + 2 * which + half))

        u = u_mat[...]
        u_twice = jnp.concatenate([u, u], axis=0)
        k_high, k_low = k_mat[0:256, :], k_mat[256:512, :]
        k_thrice = jnp.concatenate([k_high, k_high, k_low], axis=0)

        def columns(part):
            at = slice(part * 256, part * 256 + 256)
            a_buf[at, 0:256] = dot(first[at, 0:512], u_twice)
            a_buf[at, 256:512] = dot(first[at, :], k_thrice)

        def twist(part):
            for i in range(0, 128, 32):
                re_rows = slice(part * 256 + i, part * 256 + i + 32)
                im_rows = slice(part * 256 + 128 + i, part * 256 + 160 + i)
                rows = slice(part * 128 + i, part * 128 + i + 32)
                turn_re, turn_im = turn[rows, 0:256], turn[rows, 256:512]
                for which, to in enumerate((re_rows, im_rows)):
                    cols = slice(which * 256, which * 256 + 256)
                    re, im = a_buf[re_rows, cols], a_buf[im_rows, cols]
                    high, low = halves(re * turn_re - im * turn_im)
                    b_buf[to, 0:256], b_buf[to, 512:768] = high, low
                    high, low = halves(re * turn_im + im * turn_re)
                    b_buf[to, 256:512], b_buf[to, 768:1024] = high, low

        def three(data, table, rows):
            high, low = data[rows, 0:512], data[rows, 512:1024]
            return dot(high, table[0:512, :]) + dot(low, table[0:512, :]) + dot(high, table[512:1024, :])

        def product(part):
            for i in range(0, 128, 32):
                u_rows = slice(part * 256 + i, part * 256 + i + 32)
                k_rows = slice(part * 256 + 128 + i, part * 256 + 160 + i)
                to = slice(part * 128 + i, part * 128 + i + 32)
                u_re, u_im = x_buf[u_rows, 0:256], x_buf[u_rows, 256:512]
                k_re, k_im = x_buf[k_rows, 0:256], x_buf[k_rows, 256:512]
                high, low = halves(u_re * k_re - u_im * k_im)
                p_buf[to, 0:256], p_buf[to, 512:768] = high, low
                high, low = halves(u_re * k_im + u_im * k_re)
                p_buf[to, 256:512], p_buf[to, 768:1024] = high, low

        def untwist(part):
            for i in range(part * 128, part * 128 + 128, 32):
                rows = slice(i, i + 32)
                turn_re, turn_im = turn[rows, 0:256], turn[rows, 256:512]
                re, im = c_buf[rows, 0:256], c_buf[rows, 256:512]
                for at, value in ((i, re * turn_re + im * turn_im), (256 + i, im * turn_re - re * turn_im)):
                    high, low = halves(value)
                    d_buf[at : at + 32, :], d_buf[512 + at : 544 + at, :] = high, high
                    d_buf[1024 + at : 1056 + at, :] = low

        columns(0)
        columns(1)
        twist(0)
        x_buf[0:256, :] = three(b_buf, fwd, slice(0, 256))
        twist(1)
        x_buf[256:512, :] = three(b_buf, fwd, slice(256, 512))
        product(0)
        c_buf[0:128, :] = three(p_buf, bwd, slice(0, 128))
        product(1)
        c_buf[128:256, :] = three(p_buf, bwd, slice(128, 256))
        untwist(0)
        untwist(1)

        factor = byp[core * 256 + ab * CHIPS + chip]

        direct = factor * u_mat[...].astype(F32)
        y_buf[...] = dot(last[...], d_buf[...]) + direct
        at = pl.multiple_of(ab * 512, 512)
        for t in range(4):
            which, half = t // 2 * 128, t % 2 * 128
            y_send[pl.ds(at + t, CHIPS, stride=4), :] = y_buf[which : which + 128, half : half + 128]
        spread(y_send, y_recv, at, 4, send_sem.at[2 + ab], recv_sem.at[2 + ab])
        own = pl.ds(pl.multiple_of(at + chip * 4, 4), 4)
        y_recv[own, :] = y_send[own, :]

    def finish(owner, ab, half, values):
        rows, lanes = slice(half * 128, half * 128 + 128), pl.ds(pl.multiple_of(owner * 256 + ab * 128, 128), 128)
        out_ref[rows, lanes] = (values.T * gate[rows, lanes].astype(F32)).astype(BF16)

    for ab in range(2):
        drain(y_recv, 4, recv_sem.at[2 + ab])
        for half in range(2):
            y_out[ab, half * 128 : half * 128 + 128, :] = y_recv[
                pl.ds(ab * 512 + 2 * other + half, CHIPS, stride=4), :
            ]
        y_swap(ab).start()
        for half in range(2):
            finish(core, ab, half, y_recv[pl.ds(ab * 512 + 2 * core + half, CHIPS, stride=4), :])
        y_swap(ab).wait_recv()
        for half in range(2):
            finish(other, ab, half, y_in[ab, half * 128 : half * 128 + 128, :])

    post_swap.wait_send()
    for ab in range(2):
        swaps[ab].wait_send()
        y_swap(ab).wait_send()
        drain(send, 8, send_sem.at[ab])
        drain(y_send, 4, send_sem.at[2 + ab])


def on_device(consts, signal, gating, kernel, bypass):
    hbm, vmem = pl.BlockSpec(memory_space=pltpu.HBM), pl.BlockSpec(memory_space=pltpu.VMEM)
    v = pltpu.VMEM
    scratch = [
        v((256, 512), BF16), v((256, 512), BF16), v((256, 512), F32), pltpu.SMEM((512,), F32),
        *[v(c.shape, c.dtype) for c in consts],
        v((256, 512), F32), v((256, 128), F32), v((256, 128), F32), v((512, 128), F32), v((512, 128), F32),
        v((2048, 128), F32), v((2048, 128), F32), v((256, 256), BF16), v((512, 256), BF16),
        v((512, 512), F32), v((512, 1024), BF16), v((512, 512), F32), v((256, 1024), BF16), v((256, 512), F32),
        v((1536, 256), BF16), v((256, 256), F32), v((2, 256, 128), F32), v((2, 256, 128), F32), v((1024, 128), F32), v((1024, 128), F32),
        pltpu.SemaphoreType.DMA((9,)), pltpu.SemaphoreType.DMA((5,)), pltpu.SemaphoreType.DMA((5,)),
        pltpu.SemaphoreType.DMA((4,)), pltpu.SemaphoreType.DMA((4,)), pltpu.SemaphoreType.REGULAR,
    ]
    operands = [pltpu.with_memory_space_constraint(x, pltpu.HBM) for x in (signal, gating, kernel, bypass, *consts)]
    return pl.pallas_call(
        kernel_body,
        out_shape=pltpu.VMEM((256, 512), BF16),
        in_specs=[hbm] * 9,
        out_specs=vmem,
        scratch_shapes=scratch,
        compiler_params=pltpu.CompilerParams(
            collective_id=0, has_side_effects=True, vmem_limit_bytes=48 * 1024 * 1024
        ),
        name="hyena",
    )(*operands)


def solution(mesh):
    rows = P(("grp", "seq"), None)
    consts = tables()

    def whole(signal, gating, kernel, bypass):
        return jax.shard_map(
            functools.partial(on_device, [jnp.asarray(c) for c in consts]),
            mesh=mesh, in_specs=(rows, rows, rows, P()), out_specs=rows, check_vma=False,
        )(signal, gating, kernel, bypass)

    return whole
```

```python
import functools

import jax
import jax.numpy as jnp
import ml_dtypes
import numpy as np
from jax import lax
from jax.experimental import pallas as pl
from jax.experimental.pallas import tpu as pltpu
from jax.sharding import PartitionSpec as P

MESH = pl.DeviceIdType.MESH
F32 = jnp.float32
BF16 = jnp.bfloat16
ROWS = 256
CHIPS = 128
TOKENS = 65536


def hops(offset):
    dz, dx, dy = offset
    return min(dz, 8 - dz) + min(dx, 4 - dx) + min(dy, 4 - dy)


OFFSETS = [(dz, dx, dy) for dx in range(4) for dy in range(4) for dz in range(8)]
FAR_FIRST = sorted(OFFSETS[1:], key=lambda offset: -hops(offset))


def split_table(table):
    high = table.astype(ml_dtypes.bfloat16)
    low = (table - high.astype(np.float64)).astype(ml_dtypes.bfloat16)
    return high, low


def tables():
    row = np.arange(256)
    core, chip = row // CHIPS, row % CHIPS
    n1 = 32 * (chip // 16) + 16 * core + chip % 16
    index = np.arange(256)
    quarter = 4 * index - 1

    first = 2.0 * np.pi / 1024 * (quarter[:, None] * n1[None, :] % 1024)
    halved = first.reshape(2, 1, 128, 256)
    first_rows = np.concatenate([np.cos(halved), -np.sin(halved)], axis=1).reshape(512, 256)
    first_high, first_low = split_table(first_rows)
    first_all = np.concatenate([first_high, first_low, first_high], axis=1)

    turn = 2.0 * np.pi / (4 * TOKENS) * (quarter[:, None] * index[None, :] % (4 * TOKENS))
    turn_all = np.concatenate([np.cos(turn), -np.sin(turn)], axis=1).astype(np.float32)

    second = 2.0 * np.pi / 256 * (index[:, None] * index[None, :] % 256)
    cos, sin = np.cos(second), np.sin(second)
    forward = np.concatenate(split_table(np.block([[cos, -sin], [sin, cos]])), axis=0)
    backward = np.concatenate(split_table(np.block([[cos, sin], [-sin, cos]])), axis=0)

    last = np.concatenate([np.cos(first.T), -np.sin(first.T)], axis=1) / TOKENS
    last_high, last_low = split_table(last)
    last_all = np.concatenate([last_high, last_low, last_high], axis=1)
    return first_all, turn_all, forward, backward, last_all


def dot(a, b):
    return jnp.dot(a, b, preferred_element_type=F32)


def halves(x):
    high = x.astype(BF16)
    return high, (x - high.astype(F32)).astype(BF16)


def kernel_body(
    sig_hbm, gate_hbm, ker_hbm, byp_hbm, first_hbm, turn_hbm, fwd_hbm, bwd_hbm, last_hbm,
    out_ref,
    sig, gate, ker, byp, first, turn, fwd, bwd, last,
    wide, sib_u, sib_k, post_out, post_in, send, recv, u_mat, k_mat, a_buf, b_buf, x_buf, p_buf, c_buf, d_buf, y_buf, y_out, y_in, y_send, y_recv,
    load_sem, sib_send, sib_recv, send_sem, recv_sem, in_sem,
):
    grp, seq = lax.axis_index("grp"), lax.axis_index("seq")
    z, core = grp // 2, grp % 2
    other = 1 - core
    way = 1 - 2 * core
    chip = z * 16 + seq
    sibling = (z * 2 + other, seq)

    loads = [
        pltpu.make_async_copy(source, target, load_sem.at[i])
        for i, (source, target) in enumerate(
            [
                (ker_hbm, ker), (sig_hbm, sig), (first_hbm, first), (turn_hbm, turn),
                (fwd_hbm, fwd), (bwd_hbm, bwd), (last_hbm, last), (gate_hbm, gate), (byp_hbm, byp),
            ]
        )
    ]
    for load in loads[:2]:
        load.start()
    barrier = pltpu.get_barrier_semaphore()

    @pl.when(core == 1)
    def _():
        pl.semaphore_signal(barrier, inc=1, device_id=sibling, device_id_type=MESH)

    for dz, dx, dy in FAR_FIRST:
        mate = (((z + dz) & 7) * 2 + core, ((seq + 4 * dx) & 12) | ((seq + dy) & 3))
        pl.semaphore_signal(barrier, inc=1, device_id=mate, device_id_type=MESH)

    loads[0].wait()
    loads[1].wait()
    wide[...] = sig[...].astype(F32)
    near_lanes = pl.multiple_of(core * 256 + 128, 128)
    far_lanes = pl.multiple_of(other * 256 + 128, 128)

    def place(block, ab, start):
        send[pl.ds(ab * 1024 + start, CHIPS, stride=8), :] = block.T

    for half in range(2):
        rows = slice(half * 128, half * 128 + 128)
        for owner in range(2):
            lanes = slice(owner * 256, owner * 256 + 128)
            place(wide[rows, lanes], 0, 2 * owner + half)
            place(ker[rows, lanes], 0, 4 + 2 * owner + half)

    def place_near():
        for half in range(2):
            rows = slice(half * 128, half * 128 + 128)
            place(wide[rows, pl.ds(near_lanes, 128)], 1, 2 * core + half)
            place(ker[rows, pl.ds(near_lanes, 128)], 1, 4 + 2 * core + half)

    def place_sibling():
        for half in range(2):
            rows = slice(half * 128, half * 128 + 128)
            place(sib_u[rows, :], 1, 2 * other + half)
            place(sib_k[rows, :], 1, 4 + 2 * other + half)

    def spread(source, target, base, size, sends, receives, offsets=FAR_FIRST):
        for dz, dx, dy in offsets:
            to_z = (z + way * dz) & 7
            to_seq = ((seq + 4 * way * dx) & 12) | ((seq + way * dy) & 3)
            to_chip = to_z * 16 + to_seq
            pltpu.make_async_remote_copy(
                src_ref=source.at[pl.ds(pl.multiple_of(base + to_chip * size, size), size)],
                dst_ref=target.at[pl.ds(pl.multiple_of(base + chip * size, size), size)],
                send_sem=sends, recv_sem=receives,
                device_id=(to_z * 2 + core, to_seq), device_id_type=MESH,
            ).start()

    def drain(buffer, size, semaphore):
        slabs = buffer.at[pl.ds(0, (CHIPS - 1) * size)]
        pltpu.make_async_copy(slabs, slabs, semaphore).wait()

    def send_slabs(ab, offsets):
        spread(send, recv, ab * 1024, 8, send_sem.at[ab], recv_sem.at[ab], offsets)

    pl.semaphore_wait(barrier, CHIPS - core)

    @pl.when(core == 0)
    def _():
        pl.semaphore_signal(in_sem, inc=1, device_id=sibling, device_id_type=MESH)

    send_slabs(0, FAR_FIRST[:64])
    for load in loads[2:]:
        load.start()

    @pl.when(core == 1)
    def _():
        pl.semaphore_wait(in_sem, 1)

    swaps = [
        pltpu.make_async_remote_copy(
            src_ref=source.at[:, pl.ds(far_lanes, 128)], dst_ref=target, send_sem=sib_send.at[i],
            recv_sem=sib_recv.at[i], device_id=sibling, device_id_type=MESH,
        )
        for i, (source, target) in enumerate([(ker, sib_k), (wide, sib_u)])
    ]
    for swap in swaps:
        swap.start()
    send_slabs(0, FAR_FIRST[64:])
    place_near()
    for swap in swaps:
        swap.wait_recv()
    place_sibling()
    send_slabs(1, FAR_FIRST)
    for ab in range(2):
        own = pl.ds(pl.multiple_of(ab * 1024 + chip * 8, 8), 8)
        recv[own, :] = send[own, :]

    for load in loads[2:]:
        load.wait()

    def y_swap(ab):
        return pltpu.make_async_remote_copy(
            src_ref=y_out.at[ab], dst_ref=y_in.at[ab],
            send_sem=sib_send.at[2 + ab], recv_sem=sib_recv.at[2 + ab], device_id=sibling, device_id_type=MESH,
        )

    post_swap = pltpu.make_async_remote_copy(
        src_ref=post_out, dst_ref=post_in, send_sem=sib_send.at[4], recv_sem=sib_recv.at[4],
        device_id=sibling, device_id_type=MESH,
    )

    @pl.loop(0, 2)
    def _(ab):
        drain(recv, 8, recv_sem.at[ab])

        def arrived(t):
            return recv[pl.ds(ab * 1024 + t, CHIPS, stride=8), :]

        def keep(which, half, u, k):
            rows = pl.ds(pl.multiple_of(which * 128, 128), 128)
            low_rows = pl.ds(pl.multiple_of(256 + which * 128, 128), 128)
            lanes = slice(half * 128, half * 128 + 128)
            u_mat[rows, lanes] = u.astype(BF16)
            k_mat[rows, lanes], k_mat[low_rows, lanes] = halves(k)

        @pl.when(ab == 0)
        def _():
            for half in range(2):
                post_out[half * 128 : half * 128 + 128, :] = arrived(2 * other + half)
                post_out[256 + half * 128 : 384 + half * 128, :] = arrived(4 + 2 * other + half)
            post_swap.start()
            for half in range(2):
                keep(core, half, arrived(2 * core + half), arrived(4 + 2 * core + half))
            post_swap.wait_recv()
            for half in range(2):
                from_sibling = slice(half * 128, half * 128 + 128), slice(256 + half * 128, 384 + half * 128)
                keep(other, half, post_in[from_sibling[0], :], post_in[from_sibling[1], :])

        @pl.when(ab == 1)
        def _():
            for which in range(2):
                for half in range(2):
                    keep(which, half, arrived(2 * which + half), arrived(4 + 2 * which + half))

        u = u_mat[...]
        u_twice = jnp.concatenate([u, u], axis=0)
        k_high, k_low = k_mat[0:256, :], k_mat[256:512, :]
        k_thrice = jnp.concatenate([k_high, k_high, k_low], axis=0)

        def columns(part):
            at = slice(part * 256, part * 256 + 256)
            a_buf[at, 0:256] = dot(first[at, 0:512], u_twice)
            a_buf[at, 256:512] = dot(first[at, :], k_thrice)

        def twist(part):
            for i in range(0, 128, 32):
                re_rows = slice(part * 256 + i, part * 256 + i + 32)
                im_rows = slice(part * 256 + 128 + i, part * 256 + 160 + i)
                rows = slice(part * 128 + i, part * 128 + i + 32)
                turn_re, turn_im = turn[rows, 0:256], turn[rows, 256:512]
                for which, to in enumerate((re_rows, im_rows)):
                    cols = slice(which * 256, which * 256 + 256)
                    re, im = a_buf[re_rows, cols], a_buf[im_rows, cols]
                    high, low = halves(re * turn_re - im * turn_im)
                    b_buf[to, 0:256], b_buf[to, 512:768] = high, low
                    high, low = halves(re * turn_im + im * turn_re)
                    b_buf[to, 256:512], b_buf[to, 768:1024] = high, low

        def three(data, table, rows):
            high, low = data[rows, 0:512], data[rows, 512:1024]
            return dot(high, table[0:512, :]) + dot(low, table[0:512, :]) + dot(high, table[512:1024, :])

        def product(part):
            for i in range(0, 128, 32):
                u_rows = slice(part * 256 + i, part * 256 + i + 32)
                k_rows = slice(part * 256 + 128 + i, part * 256 + 160 + i)
                to = slice(part * 128 + i, part * 128 + i + 32)
                u_re, u_im = x_buf[u_rows, 0:256], x_buf[u_rows, 256:512]
                k_re, k_im = x_buf[k_rows, 0:256], x_buf[k_rows, 256:512]
                high, low = halves(u_re * k_re - u_im * k_im)
                p_buf[to, 0:256], p_buf[to, 512:768] = high, low
                high, low = halves(u_re * k_im + u_im * k_re)
                p_buf[to, 256:512], p_buf[to, 768:1024] = high, low

        def untwist(part):
            for i in range(part * 128, part * 128 + 128, 32):
                rows = slice(i, i + 32)
                turn_re, turn_im = turn[rows, 0:256], turn[rows, 256:512]
                re, im = c_buf[rows, 0:256], c_buf[rows, 256:512]
                for at, value in ((i, re * turn_re + im * turn_im), (256 + i, im * turn_re - re * turn_im)):
                    high, low = halves(value)
                    d_buf[at : at + 32, :], d_buf[512 + at : 544 + at, :] = high, high
                    d_buf[1024 + at : 1056 + at, :] = low

        columns(0)
        columns(1)
        twist(0)
        x_buf[0:256, :] = three(b_buf, fwd, slice(0, 256))
        twist(1)
        x_buf[256:512, :] = three(b_buf, fwd, slice(256, 512))
        product(0)
        c_buf[0:128, :] = three(p_buf, bwd, slice(0, 128))
        product(1)
        c_buf[128:256, :] = three(p_buf, bwd, slice(128, 256))
        untwist(0)
        untwist(1)

        factor = byp[core * 256 + ab * CHIPS + chip]

        direct = factor * u_mat[...].astype(F32)
        y_buf[...] = dot(last[...], d_buf[...]) + direct
        at = pl.multiple_of(ab * 512, 512)
        for t in range(4):
            which, half = t // 2 * 128, t % 2 * 128
            y_send[pl.ds(at + t, CHIPS, stride=4), :] = y_buf[which : which + 128, half : half + 128]
        spread(y_send, y_recv, at, 4, send_sem.at[2 + ab], recv_sem.at[2 + ab])
        own = pl.ds(pl.multiple_of(at + chip * 4, 4), 4)
        y_recv[own, :] = y_send[own, :]

    def finish(owner, ab, half, values):
        rows, lanes = slice(half * 128, half * 128 + 128), pl.ds(pl.multiple_of(owner * 256 + ab * 128, 128), 128)
        out_ref[rows, lanes] = (values.T * gate[rows, lanes].astype(F32)).astype(BF16)

    for ab in range(2):
        drain(y_recv, 4, recv_sem.at[2 + ab])
        for half in range(2):
            y_out[ab, half * 128 : half * 128 + 128, :] = y_recv[
                pl.ds(ab * 512 + 2 * other + half, CHIPS, stride=4), :
            ]
        y_swap(ab).start()
        for half in range(2):
            finish(core, ab, half, y_recv[pl.ds(ab * 512 + 2 * core + half, CHIPS, stride=4), :])
        y_swap(ab).wait_recv()
        for half in range(2):
            finish(other, ab, half, y_in[ab, half * 128 : half * 128 + 128, :])

    post_swap.wait_send()
    for ab in range(2):
        swaps[ab].wait_send()
        y_swap(ab).wait_send()
        drain(send, 8, send_sem.at[ab])
        drain(y_send, 4, send_sem.at[2 + ab])


def on_device(consts, signal, gating, kernel, bypass):
    hbm, vmem = pl.BlockSpec(memory_space=pltpu.HBM), pl.BlockSpec(memory_space=pltpu.VMEM)
    v = pltpu.VMEM
    scratch = [
        v((256, 512), BF16), v((256, 512), BF16), v((256, 512), F32), pltpu.SMEM((512,), F32),
        *[v(c.shape, c.dtype) for c in consts],
        v((256, 512), F32), v((256, 128), F32), v((256, 128), F32), v((512, 128), F32), v((512, 128), F32),
        v((2056, 128), F32), v((2056, 128), F32), v((256, 256), BF16), v((512, 256), BF16),
        v((512, 512), F32), v((512, 1024), BF16), v((512, 512), F32), v((256, 1024), BF16), v((256, 512), F32),
        v((1536, 256), BF16), v((256, 256), F32), v((2, 256, 128), F32), v((2, 256, 128), F32), v((1032, 128), F32), v((1032, 128), F32),
        pltpu.SemaphoreType.DMA((9,)), pltpu.SemaphoreType.DMA((5,)), pltpu.SemaphoreType.DMA((5,)),
        pltpu.SemaphoreType.DMA((4,)), pltpu.SemaphoreType.DMA((4,)), pltpu.SemaphoreType.REGULAR,
    ]
    operands = [pltpu.with_memory_space_constraint(x, pltpu.HBM) for x in (signal, gating, kernel, bypass, *consts)]
    return pl.pallas_call(
        kernel_body,
        out_shape=pltpu.VMEM((256, 512), BF16),
        in_specs=[hbm] * 9,
        out_specs=vmem,
        scratch_shapes=scratch,
        compiler_params=pltpu.CompilerParams(
            collective_id=0, has_side_effects=True, vmem_limit_bytes=48 * 1024 * 1024
        ),
        name="hyena",
    )(*operands)


def solution(mesh):
    rows = P(("grp", "seq"), None)
    consts = tables()

    def whole(signal, gating, kernel, bypass):
        return jax.shard_map(
            functools.partial(on_device, [jnp.asarray(c) for c in consts]),
            mesh=mesh, in_specs=(rows, rows, rows, P()), out_specs=rows, check_vma=False,
        )(signal, gating, kernel, bypass)

    return whole
```

```python
import functools

import jax
import jax.numpy as jnp
import ml_dtypes
import numpy as np
from jax import lax
from jax.experimental import pallas as pl
from jax.experimental.pallas import tpu as pltpu
from jax.sharding import PartitionSpec as P

MESH = pl.DeviceIdType.MESH
F32 = jnp.float32
BF16 = jnp.bfloat16
ROWS = 256
CHIPS = 128
TOKENS = 65536


def hops(offset):
    dz, dx, dy = offset
    return min(dz, 8 - dz) + min(dx, 4 - dx) + min(dy, 4 - dy)


OFFSETS = [(dz, dx, dy) for dx in range(4) for dy in range(4) for dz in range(8)]
FAR_FIRST = sorted(OFFSETS[1:], key=lambda offset: -hops(offset))


def split_table(table):
    high = table.astype(ml_dtypes.bfloat16)
    low = (table - high.astype(np.float64)).astype(ml_dtypes.bfloat16)
    return high, low


def tables():
    row = np.arange(256)
    core, chip = row // CHIPS, row % CHIPS
    n1 = 32 * (chip // 16) + 16 * core + chip % 16
    index = np.arange(256)
    quarter = 4 * index - 1

    first = 2.0 * np.pi / 1024 * (quarter[:, None] * n1[None, :] % 1024)
    halved = first.reshape(2, 1, 128, 256)
    first_rows = np.concatenate([np.cos(halved), -np.sin(halved)], axis=1).reshape(512, 256)
    first_high, first_low = split_table(first_rows)
    first_all = np.concatenate([first_high, first_low, first_high], axis=1)

    turn = 2.0 * np.pi / (4 * TOKENS) * (quarter[:, None] * index[None, :] % (4 * TOKENS))
    turn_all = np.concatenate([np.cos(turn), -np.sin(turn)], axis=1).astype(np.float32)

    second = 2.0 * np.pi / 256 * (index[:, None] * index[None, :] % 256)
    cos, sin = np.cos(second), np.sin(second)
    forward = np.concatenate(split_table(np.block([[cos, -sin], [sin, cos]])), axis=0)
    backward = np.concatenate(split_table(np.block([[cos, sin], [-sin, cos]])), axis=0)

    last = np.concatenate([np.cos(first.T), -np.sin(first.T)], axis=1) / TOKENS
    last_high, last_low = split_table(last)
    last_all = np.concatenate([last_high, last_low, last_high], axis=1)
    return first_all, turn_all, forward, backward, last_all


def dot(a, b):
    return jnp.dot(a, b, preferred_element_type=F32)


def halves(x):
    high = x.astype(BF16)
    return high, (x - high.astype(F32)).astype(BF16)


def kernel_body(
    sig_hbm, gate_hbm, ker_hbm, byp_hbm, first_hbm, turn_hbm, fwd_hbm, bwd_hbm, last_hbm,
    out_ref,
    sig, gate, ker, byp, first, turn, fwd, bwd, last,
    wide, sib_u, sib_k, post_out, post_in, send, recv, u_mat, k_mat, a_buf, b_buf, x_buf, p_buf, c_buf, d_buf, y_buf, y_out, y_in, y_send, y_recv,
    load_sem, sib_send, sib_recv, send_sem, recv_sem, in_sem,
):
    grp, seq = lax.axis_index("grp"), lax.axis_index("seq")
    z, core = grp // 2, grp % 2
    other = 1 - core
    way = 1 - 2 * core
    chip = z * 16 + seq
    sibling = (z * 2 + other, seq)

    loads = [
        pltpu.make_async_copy(source, target, load_sem.at[i])
        for i, (source, target) in enumerate(
            [
                (ker_hbm, ker), (sig_hbm, sig), (first_hbm, first), (turn_hbm, turn),
                (fwd_hbm, fwd), (bwd_hbm, bwd), (last_hbm, last), (gate_hbm, gate), (byp_hbm, byp),
            ]
        )
    ]
    for load in loads[:2]:
        load.start()
    barrier = pltpu.get_barrier_semaphore()

    @pl.when(core == 1)
    def _():
        pl.semaphore_signal(barrier, inc=1, device_id=sibling, device_id_type=MESH)

    for dz, dx, dy in FAR_FIRST:
        mate = (((z + dz) & 7) * 2 + core, ((seq + 4 * dx) & 12) | ((seq + dy) & 3))
        pl.semaphore_signal(barrier, inc=1, device_id=mate, device_id_type=MESH)

    loads[0].wait()
    loads[1].wait()
    wide[...] = sig[...].astype(F32)
    near_lanes = pl.multiple_of(core * 256 + 128, 128)
    far_lanes = pl.multiple_of(other * 256 + 128, 128)

    def place(block, ab, start):
        send[pl.ds(ab * 1024 + start, CHIPS, stride=8), :] = block.T

    for half in range(2):
        rows = slice(half * 128, half * 128 + 128)
        for owner in range(2):
            lanes = slice(owner * 256, owner * 256 + 128)
            place(wide[rows, lanes], 0, 2 * owner + half)
            place(ker[rows, lanes], 0, 4 + 2 * owner + half)

    def place_near():
        for half in range(2):
            rows = slice(half * 128, half * 128 + 128)
            place(wide[rows, pl.ds(near_lanes, 128)], 1, 2 * core + half)
            place(ker[rows, pl.ds(near_lanes, 128)], 1, 4 + 2 * core + half)

    def place_sibling():
        for half in range(2):
            rows = slice(half * 128, half * 128 + 128)
            place(sib_u[rows, :], 1, 2 * other + half)
            place(sib_k[rows, :], 1, 4 + 2 * other + half)

    def spread(source, target, base, size, sends, receives, offsets=FAR_FIRST):
        for dz, dx, dy in offsets:
            to_z = (z + way * dz) & 7
            to_seq = ((seq + 4 * way * dx) & 12) | ((seq + way * dy) & 3)
            to_chip = to_z * 16 + to_seq
            pltpu.make_async_remote_copy(
                src_ref=source.at[pl.ds(pl.multiple_of(base + to_chip * size, size), size)],
                dst_ref=target.at[pl.ds(pl.multiple_of(base + chip * size, size), size)],
                send_sem=sends, recv_sem=receives,
                device_id=(to_z * 2 + core, to_seq), device_id_type=MESH,
            ).start()

    def drain(buffer, size, semaphore):
        slabs = buffer.at[pl.ds(0, (CHIPS - 1) * size)]
        pltpu.make_async_copy(slabs, slabs, semaphore).wait()

    def send_slabs(ab, offsets):
        spread(send, recv, ab * 1024, 8, send_sem.at[ab], recv_sem.at[ab], offsets)

    pl.semaphore_wait(barrier, CHIPS - core)

    @pl.when(core == 0)
    def _():
        pl.semaphore_signal(in_sem, inc=1, device_id=sibling, device_id_type=MESH)

    send_slabs(0, FAR_FIRST[:64])
    for load in loads[2:]:
        load.start()

    @pl.when(core == 1)
    def _():
        pl.semaphore_wait(in_sem, 1)

    swaps = [
        pltpu.make_async_remote_copy(
            src_ref=source.at[:, pl.ds(far_lanes, 128)], dst_ref=target, send_sem=sib_send.at[i],
            recv_sem=sib_recv.at[i], device_id=sibling, device_id_type=MESH,
        )
        for i, (source, target) in enumerate([(ker, sib_k), (wide, sib_u)])
    ]
    for swap in swaps:
        swap.start()
    send_slabs(0, FAR_FIRST[64:])
    place_near()
    for swap in swaps:
        swap.wait_recv()
    place_sibling()
    send_slabs(1, FAR_FIRST)
    for ab in range(2):
        own = pl.ds(pl.multiple_of(ab * 1024 + chip * 8, 8), 8)
        recv[own, :] = send[own, :]

    for load in loads[2:]:
        load.wait()

    def y_swap(ab):
        return pltpu.make_async_remote_copy(
            src_ref=y_out.at[ab], dst_ref=y_in.at[ab],
            send_sem=sib_send.at[2 + ab], recv_sem=sib_recv.at[2 + ab], device_id=sibling, device_id_type=MESH,
        )

    post_swap = pltpu.make_async_remote_copy(
        src_ref=post_out, dst_ref=post_in, send_sem=sib_send.at[4], recv_sem=sib_recv.at[4],
        device_id=sibling, device_id_type=MESH,
    )

    @pl.loop(0, 2)
    def _(ab):
        drain(recv, 8, recv_sem.at[ab])

        def arrived(t):
            return recv[pl.ds(ab * 1024 + t, CHIPS, stride=8), :]

        def keep(which, half, u, k):
            rows = pl.ds(pl.multiple_of(which * 128, 128), 128)
            low_rows = pl.ds(pl.multiple_of(256 + which * 128, 128), 128)
            lanes = slice(half * 128, half * 128 + 128)
            u_mat[rows, lanes] = u.astype(BF16)
            k_mat[rows, lanes], k_mat[low_rows, lanes] = halves(k)

        @pl.when(ab == 0)
        def _():
            for half in range(2):
                post_out[half * 128 : half * 128 + 128, :] = arrived(2 * other + half)
                post_out[256 + half * 128 : 384 + half * 128, :] = arrived(4 + 2 * other + half)
            post_swap.start()
            for half in range(2):
                keep(core, half, arrived(2 * core + half), arrived(4 + 2 * core + half))
            post_swap.wait_recv()
            for half in range(2):
                from_sibling = slice(half * 128, half * 128 + 128), slice(256 + half * 128, 384 + half * 128)
                keep(other, half, post_in[from_sibling[0], :], post_in[from_sibling[1], :])

        @pl.when(ab == 1)
        def _():
            for which in range(2):
                for half in range(2):
                    keep(which, half, arrived(2 * which + half), arrived(4 + 2 * which + half))

        u = u_mat[...]
        u_twice = jnp.concatenate([u, u], axis=0)
        k_high, k_low = k_mat[0:256, :], k_mat[256:512, :]
        k_thrice = jnp.concatenate([k_high, k_high, k_low], axis=0)

        def columns(part):
            at = slice(part * 256, part * 256 + 256)
            a_buf[at, 0:256] = dot(first[at, 0:512], u_twice)
            a_buf[at, 256:512] = dot(first[at, :], k_thrice)

        def twist(part):
            for i in range(0, 128, 32):
                re_rows = slice(part * 256 + i, part * 256 + i + 32)
                im_rows = slice(part * 256 + 128 + i, part * 256 + 160 + i)
                rows = slice(part * 128 + i, part * 128 + i + 32)
                turn_re, turn_im = turn[rows, 0:256], turn[rows, 256:512]
                for which, to in enumerate((re_rows, im_rows)):
                    cols = slice(which * 256, which * 256 + 256)
                    re, im = a_buf[re_rows, cols], a_buf[im_rows, cols]
                    high, low = halves(re * turn_re - im * turn_im)
                    b_buf[to, 0:256], b_buf[to, 512:768] = high, low
                    high, low = halves(re * turn_im + im * turn_re)
                    b_buf[to, 256:512], b_buf[to, 768:1024] = high, low

        def three(data, table, rows):
            high, low = data[rows, 0:512], data[rows, 512:1024]
            return dot(high, table[0:512, :]) + dot(low, table[0:512, :]) + dot(high, table[512:1024, :])

        def product(part):
            for i in range(0, 128, 32):
                u_rows = slice(part * 256 + i, part * 256 + i + 32)
                k_rows = slice(part * 256 + 128 + i, part * 256 + 160 + i)
                to = slice(part * 128 + i, part * 128 + i + 32)
                u_re, u_im = x_buf[u_rows, 0:256], x_buf[u_rows, 256:512]
                k_re, k_im = x_buf[k_rows, 0:256], x_buf[k_rows, 256:512]
                high, low = halves(u_re * k_re - u_im * k_im)
                p_buf[to, 0:256], p_buf[to, 512:768] = high, low
                high, low = halves(u_re * k_im + u_im * k_re)
                p_buf[to, 256:512], p_buf[to, 768:1024] = high, low

        def untwist(part):
            for i in range(part * 128, part * 128 + 128, 32):
                rows = slice(i, i + 32)
                turn_re, turn_im = turn[rows, 0:256], turn[rows, 256:512]
                re, im = c_buf[rows, 0:256], c_buf[rows, 256:512]
                for at, value in ((i, re * turn_re + im * turn_im), (256 + i, im * turn_re - re * turn_im)):
                    high, low = halves(value)
                    d_buf[at : at + 32, :], d_buf[512 + at : 544 + at, :] = high, high
                    d_buf[1024 + at : 1056 + at, :] = low

        columns(0)
        twist(0)
        columns(1)
        x_buf[0:256, :] = three(b_buf, fwd, slice(0, 256))
        twist(1)
        x_buf[256:512, :] = three(b_buf, fwd, slice(256, 512))
        product(0)
        c_buf[0:128, :] = three(p_buf, bwd, slice(0, 128))
        product(1)
        untwist(0)
        c_buf[128:256, :] = three(p_buf, bwd, slice(128, 256))
        untwist(1)

        factor = byp[core * 256 + ab * CHIPS + chip]

        direct = factor * u_mat[...].astype(F32)
        y_buf[...] = dot(last[...], d_buf[...]) + direct
        at = pl.multiple_of(ab * 512, 512)
        for t in range(4):
            which, half = t // 2 * 128, t % 2 * 128
            y_send[pl.ds(at + t, CHIPS, stride=4), :] = y_buf[which : which + 128, half : half + 128]
        spread(y_send, y_recv, at, 4, send_sem.at[2 + ab], recv_sem.at[2 + ab])
        own = pl.ds(pl.multiple_of(at + chip * 4, 4), 4)
        y_recv[own, :] = y_send[own, :]

    def finish(owner, ab, half, values):
        rows, lanes = slice(half * 128, half * 128 + 128), pl.ds(pl.multiple_of(owner * 256 + ab * 128, 128), 128)
        out_ref[rows, lanes] = (values.T * gate[rows, lanes].astype(F32)).astype(BF16)

    for ab in range(2):
        drain(y_recv, 4, recv_sem.at[2 + ab])
        for half in range(2):
            y_out[ab, half * 128 : half * 128 + 128, :] = y_recv[
                pl.ds(ab * 512 + 2 * other + half, CHIPS, stride=4), :
            ]
        y_swap(ab).start()
        for half in range(2):
            finish(core, ab, half, y_recv[pl.ds(ab * 512 + 2 * core + half, CHIPS, stride=4), :])
        y_swap(ab).wait_recv()
        for half in range(2):
            finish(other, ab, half, y_in[ab, half * 128 : half * 128 + 128, :])

    post_swap.wait_send()
    for ab in range(2):
        swaps[ab].wait_send()
        y_swap(ab).wait_send()
        drain(send, 8, send_sem.at[ab])
        drain(y_send, 4, send_sem.at[2 + ab])


def on_device(consts, signal, gating, kernel, bypass):
    hbm, vmem = pl.BlockSpec(memory_space=pltpu.HBM), pl.BlockSpec(memory_space=pltpu.VMEM)
    v = pltpu.VMEM
    scratch = [
        v((256, 512), BF16), v((256, 512), BF16), v((256, 512), F32), pltpu.SMEM((512,), F32),
        *[v(c.shape, c.dtype) for c in consts],
        v((256, 512), F32), v((256, 128), F32), v((256, 128), F32), v((512, 128), F32), v((512, 128), F32),
        v((2056, 128), F32), v((2056, 128), F32), v((256, 256), BF16), v((512, 256), BF16),
        v((512, 512), F32), v((512, 1024), BF16), v((512, 512), F32), v((256, 1024), BF16), v((256, 512), F32),
        v((1536, 256), BF16), v((256, 256), F32), v((2, 256, 128), F32), v((2, 256, 128), F32), v((1032, 128), F32), v((1032, 128), F32),
        pltpu.SemaphoreType.DMA((9,)), pltpu.SemaphoreType.DMA((5,)), pltpu.SemaphoreType.DMA((5,)),
        pltpu.SemaphoreType.DMA((4,)), pltpu.SemaphoreType.DMA((4,)), pltpu.SemaphoreType.REGULAR,
    ]
    operands = [pltpu.with_memory_space_constraint(x, pltpu.HBM) for x in (signal, gating, kernel, bypass, *consts)]
    return pl.pallas_call(
        kernel_body,
        out_shape=pltpu.VMEM((256, 512), BF16),
        in_specs=[hbm] * 9,
        out_specs=vmem,
        scratch_shapes=scratch,
        compiler_params=pltpu.CompilerParams(
            collective_id=0, has_side_effects=True, vmem_limit_bytes=48 * 1024 * 1024
        ),
        name="hyena",
    )(*operands)


def solution(mesh):
    rows = P(("grp", "seq"), None)
    consts = tables()

    def whole(signal, gating, kernel, bypass):
        return jax.shard_map(
            functools.partial(on_device, [jnp.asarray(c) for c in consts]),
            mesh=mesh, in_specs=(rows, rows, rows, P()), out_specs=rows, check_vma=False,
        )(signal, gating, kernel, bypass)

    return whole
```

```python
import functools

import jax
import jax.numpy as jnp
import ml_dtypes
import numpy as np
from jax import lax
from jax.experimental import pallas as pl
from jax.experimental.pallas import tpu as pltpu
from jax.sharding import PartitionSpec as P

MESH = pl.DeviceIdType.MESH
F32 = jnp.float32
BF16 = jnp.bfloat16
ROWS = 256
CHIPS = 128
TOKENS = 65536


def hops(offset):
    dz, dx, dy = offset
    return min(dz, 8 - dz) + min(dx, 4 - dx) + min(dy, 4 - dy)


OFFSETS = [(dz, dx, dy) for dx in range(4) for dy in range(4) for dz in range(8)]
FAR_FIRST = sorted(OFFSETS[1:], key=lambda offset: -hops(offset))


def alternate(offsets):
    turns = [[], [], []]
    for offset in offsets:
        turns[0 if 0 < offset[0] < 4 else 1 if offset[0] > 4 else 2].append(offset)
    longest = max(len(turn) for turn in turns)
    return [turn[i] for i in range(longest) for turn in turns if i < len(turn)]


ALTERNATE = alternate(FAR_FIRST)


def split_table(table):
    high = table.astype(ml_dtypes.bfloat16)
    low = (table - high.astype(np.float64)).astype(ml_dtypes.bfloat16)
    return high, low


def tables():
    row = np.arange(256)
    core, chip = row // CHIPS, row % CHIPS
    n1 = 32 * (chip // 16) + 16 * core + chip % 16
    index = np.arange(256)
    quarter = 4 * index - 1

    first = 2.0 * np.pi / 1024 * (quarter[:, None] * n1[None, :] % 1024)
    halved = first.reshape(2, 1, 128, 256)
    first_rows = np.concatenate([np.cos(halved), -np.sin(halved)], axis=1).reshape(512, 256)
    first_high, first_low = split_table(first_rows)
    first_all = np.concatenate([first_high, first_low, first_high], axis=1)

    turn = 2.0 * np.pi / (4 * TOKENS) * (quarter[:, None] * index[None, :] % (4 * TOKENS))
    turn_all = np.concatenate([np.cos(turn), -np.sin(turn)], axis=1).astype(np.float32)

    second = 2.0 * np.pi / 256 * (index[:, None] * index[None, :] % 256)
    cos, sin = np.cos(second), np.sin(second)
    forward = np.concatenate(split_table(np.block([[cos, -sin], [sin, cos]])), axis=0)
    backward = np.concatenate(split_table(np.block([[cos, sin], [-sin, cos]])), axis=0)

    last = np.concatenate([np.cos(first.T), -np.sin(first.T)], axis=1) / TOKENS
    last_high, last_low = split_table(last)
    last_all = np.concatenate([last_high, last_low, last_high], axis=1)
    return first_all, turn_all, forward, backward, last_all


def dot(a, b):
    return jnp.dot(a, b, preferred_element_type=F32)


def halves(x):
    high = x.astype(BF16)
    return high, (x - high.astype(F32)).astype(BF16)


def kernel_body(
    sig_hbm, gate_hbm, ker_hbm, byp_hbm, first_hbm, turn_hbm, fwd_hbm, bwd_hbm, last_hbm,
    out_ref,
    sig, gate, ker, byp, first, turn, fwd, bwd, last,
    wide, sib_u, sib_k, post_out, post_in, send, recv, u_mat, k_mat, a_buf, b_buf, x_buf, p_buf, c_buf, d_buf, y_buf, y_out, y_in, y_send, y_recv,
    load_sem, sib_send, sib_recv, send_sem, recv_sem, in_sem,
):
    grp, seq = lax.axis_index("grp"), lax.axis_index("seq")
    z, core = grp // 2, grp % 2
    other = 1 - core
    way = 1 - 2 * core
    chip = z * 16 + seq
    sibling = (z * 2 + other, seq)

    loads = [
        pltpu.make_async_copy(source, target, load_sem.at[i])
        for i, (source, target) in enumerate(
            [
                (ker_hbm, ker), (sig_hbm, sig), (first_hbm, first), (turn_hbm, turn),
                (fwd_hbm, fwd), (bwd_hbm, bwd), (last_hbm, last), (gate_hbm, gate), (byp_hbm, byp),
            ]
        )
    ]
    for load in loads[:2]:
        load.start()
    barrier = pltpu.get_barrier_semaphore()

    @pl.when(core == 1)
    def _():
        pl.semaphore_signal(barrier, inc=1, device_id=sibling, device_id_type=MESH)

    for dz, dx, dy in FAR_FIRST:
        mate = (((z + dz) & 7) * 2 + core, ((seq + 4 * dx) & 12) | ((seq + dy) & 3))
        pl.semaphore_signal(barrier, inc=1, device_id=mate, device_id_type=MESH)

    loads[0].wait()
    loads[1].wait()
    wide[...] = sig[...].astype(F32)
    near_lanes = pl.multiple_of(core * 256 + 128, 128)
    far_lanes = pl.multiple_of(other * 256 + 128, 128)

    def place(block, ab, start):
        send[pl.ds(ab * 1024 + start, CHIPS, stride=8), :] = block.T

    for half in range(2):
        rows = slice(half * 128, half * 128 + 128)
        for owner in range(2):
            lanes = slice(owner * 256, owner * 256 + 128)
            place(wide[rows, lanes], 0, 2 * owner + half)
            place(ker[rows, lanes], 0, 4 + 2 * owner + half)

    def place_near():
        for half in range(2):
            rows = slice(half * 128, half * 128 + 128)
            place(wide[rows, pl.ds(near_lanes, 128)], 1, 2 * core + half)
            place(ker[rows, pl.ds(near_lanes, 128)], 1, 4 + 2 * core + half)

    def place_sibling():
        for half in range(2):
            rows = slice(half * 128, half * 128 + 128)
            place(sib_u[rows, :], 1, 2 * other + half)
            place(sib_k[rows, :], 1, 4 + 2 * other + half)

    def spread(source, target, base, size, sends, receives, offsets=FAR_FIRST):
        for dz, dx, dy in offsets:
            to_z = (z + way * dz) & 7
            to_seq = ((seq + 4 * way * dx) & 12) | ((seq + way * dy) & 3)
            to_chip = to_z * 16 + to_seq
            pltpu.make_async_remote_copy(
                src_ref=source.at[pl.ds(pl.multiple_of(base + to_chip * size, size), size)],
                dst_ref=target.at[pl.ds(pl.multiple_of(base + chip * size, size), size)],
                send_sem=sends, recv_sem=receives,
                device_id=(to_z * 2 + core, to_seq), device_id_type=MESH,
            ).start()

    def drain(buffer, size, semaphore):
        slabs = buffer.at[pl.ds(0, (CHIPS - 1) * size)]
        pltpu.make_async_copy(slabs, slabs, semaphore).wait()

    def send_slabs(ab, offsets):
        spread(send, recv, ab * 1024, 8, send_sem.at[ab], recv_sem.at[ab], offsets)

    pl.semaphore_wait(barrier, CHIPS - core)

    @pl.when(core == 0)
    def _():
        pl.semaphore_signal(in_sem, inc=1, device_id=sibling, device_id_type=MESH)

    send_slabs(0, FAR_FIRST[:64])
    for load in loads[2:]:
        load.start()

    @pl.when(core == 1)
    def _():
        pl.semaphore_wait(in_sem, 1)

    swaps = [
        pltpu.make_async_remote_copy(
            src_ref=source.at[:, pl.ds(far_lanes, 128)], dst_ref=target, send_sem=sib_send.at[i],
            recv_sem=sib_recv.at[i], device_id=sibling, device_id_type=MESH,
        )
        for i, (source, target) in enumerate([(ker, sib_k), (wide, sib_u)])
    ]
    for swap in swaps:
        swap.start()
    send_slabs(0, FAR_FIRST[64:])
    place_near()
    for swap in swaps:
        swap.wait_recv()
    place_sibling()
    send_slabs(1, FAR_FIRST)
    for ab in range(2):
        own = pl.ds(pl.multiple_of(ab * 1024 + chip * 8, 8), 8)
        recv[own, :] = send[own, :]

    for load in loads[2:]:
        load.wait()

    def y_swap(ab):
        return pltpu.make_async_remote_copy(
            src_ref=y_out.at[ab], dst_ref=y_in.at[ab],
            send_sem=sib_send.at[2 + ab], recv_sem=sib_recv.at[2 + ab], device_id=sibling, device_id_type=MESH,
        )

    post_swap = pltpu.make_async_remote_copy(
        src_ref=post_out, dst_ref=post_in, send_sem=sib_send.at[4], recv_sem=sib_recv.at[4],
        device_id=sibling, device_id_type=MESH,
    )

    @pl.loop(0, 2)
    def _(ab):
        drain(recv, 8, recv_sem.at[ab])

        def arrived(t):
            return recv[pl.ds(ab * 1024 + t, CHIPS, stride=8), :]

        def keep(which, half, u, k):
            rows = pl.ds(pl.multiple_of(which * 128, 128), 128)
            low_rows = pl.ds(pl.multiple_of(256 + which * 128, 128), 128)
            lanes = slice(half * 128, half * 128 + 128)
            u_mat[rows, lanes] = u.astype(BF16)
            k_mat[rows, lanes], k_mat[low_rows, lanes] = halves(k)

        @pl.when(ab == 0)
        def _():
            for half in range(2):
                post_out[half * 128 : half * 128 + 128, :] = arrived(2 * other + half)
                post_out[256 + half * 128 : 384 + half * 128, :] = arrived(4 + 2 * other + half)
            post_swap.start()
            for half in range(2):
                keep(core, half, arrived(2 * core + half), arrived(4 + 2 * core + half))
            post_swap.wait_recv()
            for half in range(2):
                from_sibling = slice(half * 128, half * 128 + 128), slice(256 + half * 128, 384 + half * 128)
                keep(other, half, post_in[from_sibling[0], :], post_in[from_sibling[1], :])

        @pl.when(ab == 1)
        def _():
            for which in range(2):
                for half in range(2):
                    keep(which, half, arrived(2 * which + half), arrived(4 + 2 * which + half))

        u = u_mat[...]
        u_twice = jnp.concatenate([u, u], axis=0)
        k_high, k_low = k_mat[0:256, :], k_mat[256:512, :]
        k_thrice = jnp.concatenate([k_high, k_high, k_low], axis=0)

        def columns(part):
            at = slice(part * 256, part * 256 + 256)
            a_buf[at, 0:256] = dot(first[at, 0:512], u_twice)
            a_buf[at, 256:512] = dot(first[at, :], k_thrice)

        def twist(part):
            for i in range(0, 128, 32):
                re_rows = slice(part * 256 + i, part * 256 + i + 32)
                im_rows = slice(part * 256 + 128 + i, part * 256 + 160 + i)
                rows = slice(part * 128 + i, part * 128 + i + 32)
                turn_re, turn_im = turn[rows, 0:256], turn[rows, 256:512]
                for which, to in enumerate((re_rows, im_rows)):
                    cols = slice(which * 256, which * 256 + 256)
                    re, im = a_buf[re_rows, cols], a_buf[im_rows, cols]
                    high, low = halves(re * turn_re - im * turn_im)
                    b_buf[to, 0:256], b_buf[to, 512:768] = high, low
                    high, low = halves(re * turn_im + im * turn_re)
                    b_buf[to, 256:512], b_buf[to, 768:1024] = high, low

        def three(data, table, rows):
            high, low = data[rows, 0:512], data[rows, 512:1024]
            return dot(high, table[0:512, :]) + dot(low, table[0:512, :]) + dot(high, table[512:1024, :])

        def product(part):
            for i in range(0, 128, 32):
                u_rows = slice(part * 256 + i, part * 256 + i + 32)
                k_rows = slice(part * 256 + 128 + i, part * 256 + 160 + i)
                to = slice(part * 128 + i, part * 128 + i + 32)
                u_re, u_im = x_buf[u_rows, 0:256], x_buf[u_rows, 256:512]
                k_re, k_im = x_buf[k_rows, 0:256], x_buf[k_rows, 256:512]
                high, low = halves(u_re * k_re - u_im * k_im)
                p_buf[to, 0:256], p_buf[to, 512:768] = high, low
                high, low = halves(u_re * k_im + u_im * k_re)
                p_buf[to, 256:512], p_buf[to, 768:1024] = high, low

        def untwist(part):
            for i in range(part * 128, part * 128 + 128, 32):
                rows = slice(i, i + 32)
                turn_re, turn_im = turn[rows, 0:256], turn[rows, 256:512]
                re, im = c_buf[rows, 0:256], c_buf[rows, 256:512]
                for at, value in ((i, re * turn_re + im * turn_im), (256 + i, im * turn_re - re * turn_im)):
                    high, low = halves(value)
                    d_buf[at : at + 32, :], d_buf[512 + at : 544 + at, :] = high, high
                    d_buf[1024 + at : 1056 + at, :] = low

        columns(0)
        columns(1)
        twist(0)
        x_buf[0:256, :] = three(b_buf, fwd, slice(0, 256))
        twist(1)
        x_buf[256:512, :] = three(b_buf, fwd, slice(256, 512))
        product(0)
        c_buf[0:128, :] = three(p_buf, bwd, slice(0, 128))
        product(1)
        c_buf[128:256, :] = three(p_buf, bwd, slice(128, 256))
        untwist(0)
        untwist(1)

        factor = byp[core * 256 + ab * CHIPS + chip]

        direct = factor * u_mat[...].astype(F32)
        y_buf[...] = dot(last[...], d_buf[...]) + direct
        at = pl.multiple_of(ab * 512, 512)
        for t in range(4):
            which, half = t // 2 * 128, t % 2 * 128
            y_send[pl.ds(at + t, CHIPS, stride=4), :] = y_buf[which : which + 128, half : half + 128]
        spread(y_send, y_recv, at, 4, send_sem.at[2 + ab], recv_sem.at[2 + ab], ALTERNATE)
        own = pl.ds(pl.multiple_of(at + chip * 4, 4), 4)
        y_recv[own, :] = y_send[own, :]

    def finish(owner, ab, half, values):
        rows, lanes = slice(half * 128, half * 128 + 128), pl.ds(pl.multiple_of(owner * 256 + ab * 128, 128), 128)
        out_ref[rows, lanes] = (values.T * gate[rows, lanes].astype(F32)).astype(BF16)

    for ab in range(2):
        drain(y_recv, 4, recv_sem.at[2 + ab])
        for half in range(2):
            y_out[ab, half * 128 : half * 128 + 128, :] = y_recv[
                pl.ds(ab * 512 + 2 * other + half, CHIPS, stride=4), :
            ]
        y_swap(ab).start()
        for half in range(2):
            finish(core, ab, half, y_recv[pl.ds(ab * 512 + 2 * core + half, CHIPS, stride=4), :])
        y_swap(ab).wait_recv()
        for half in range(2):
            finish(other, ab, half, y_in[ab, half * 128 : half * 128 + 128, :])

    post_swap.wait_send()
    for ab in range(2):
        swaps[ab].wait_send()
        y_swap(ab).wait_send()
        drain(send, 8, send_sem.at[ab])
        drain(y_send, 4, send_sem.at[2 + ab])


def on_device(consts, signal, gating, kernel, bypass):
    hbm, vmem = pl.BlockSpec(memory_space=pltpu.HBM), pl.BlockSpec(memory_space=pltpu.VMEM)
    v = pltpu.VMEM
    scratch = [
        v((256, 512), BF16), v((256, 512), BF16), v((256, 512), F32), pltpu.SMEM((512,), F32),
        *[v(c.shape, c.dtype) for c in consts],
        v((256, 512), F32), v((256, 128), F32), v((256, 128), F32), v((512, 128), F32), v((512, 128), F32),
        v((2056, 128), F32), v((2056, 128), F32), v((256, 256), BF16), v((512, 256), BF16),
        v((512, 512), F32), v((512, 1024), BF16), v((512, 512), F32), v((256, 1024), BF16), v((256, 512), F32),
        v((1536, 256), BF16), v((256, 256), F32), v((2, 256, 128), F32), v((2, 256, 128), F32), v((1032, 128), F32), v((1032, 128), F32),
        pltpu.SemaphoreType.DMA((9,)), pltpu.SemaphoreType.DMA((5,)), pltpu.SemaphoreType.DMA((5,)),
        pltpu.SemaphoreType.DMA((4,)), pltpu.SemaphoreType.DMA((4,)), pltpu.SemaphoreType.REGULAR,
    ]
    operands = [pltpu.with_memory_space_constraint(x, pltpu.HBM) for x in (signal, gating, kernel, bypass, *consts)]
    return pl.pallas_call(
        kernel_body,
        out_shape=pltpu.VMEM((256, 512), BF16),
        in_specs=[hbm] * 9,
        out_specs=vmem,
        scratch_shapes=scratch,
        compiler_params=pltpu.CompilerParams(
            collective_id=0, has_side_effects=True, vmem_limit_bytes=48 * 1024 * 1024
        ),
        name="hyena",
    )(*operands)


def solution(mesh):
    rows = P(("grp", "seq"), None)
    consts = tables()

    def whole(signal, gating, kernel, bypass):
        return jax.shard_map(
            functools.partial(on_device, [jnp.asarray(c) for c in consts]),
            mesh=mesh, in_specs=(rows, rows, rows, P()), out_specs=rows, check_vma=False,
        )(signal, gating, kernel, bypass)

    return whole
```
